128 devices in a mesh: img: 8 (over y, core), txt: 16 (over x, z).
Axes of the slice: x: 4, y: 4, z: 4, core: 2. Of those that a mesh axis runs over, the one named last changes fastest.
Arguments:
- features: bfloat16 [128, 64, 8192], P('txt'), may hold values from -6 to 6
- tile_count: int32 [128], P('txt'), may hold values from 1 to 4
- kv_weight: bfloat16 [8192, 2, 1024], P(None, None, 'img'), may hold values from -0.0625 to 0.0625
- queries: bfloat16 [24576, 8192], P('txt', 'img'), may hold values from -240 to 240
- out_grad: bfloat16 [24576, 8192], P('txt', 'img'), may hold values from -6 to 6
- image_ids: int32 [192, 2], P('txt'), may hold values from 0 to 127, as said below
- text_len: int32 [192], P('txt'), may hold values from 16 to 128
Outputs:
- attn_out: bfloat16 [24576, 8192], P('txt', 'img')
- query_grad: bfloat16 [24576, 8192], P('txt', 'img')
- weight_grad: float32 [8192, 2, 1024], P('txt', None, 'img')
The draws below stay inside these ranges and needn't reach their ends.
Inputs may be any that keep to these rules, and one draw needn't show every extreme that they name: `image_ids`: each 12 consecutive sequences form one text shard; among its 24 entries at most 2 name images of one image shard (8 consecutive ids), and some image shard is named exactly 2 times there.
All inputs are finite; a program needn't handle non-finite values.
Results may differ from the reference program's by a relative error of at most 0.018.
The reference program's roundings to bfloat16 on the way (of `keyval`, `probs_low`, `scores_low` and `pair_grad`) count: a program that leaves them out, or rounds other values in their place, can miss the bound.
Values may be sent and summed in bfloat16 or wider, within the bound.
No kernel may reach another device: no remote copies, remote signals or barrier semaphores. Data moves between devices by JAX's collectives and lax.ppermute only.
A program may use at most 192 MiB of HBM per device.

```python
import math
import jax
import jax.numpy as jnp
from jax import lax

HEADS = 64
KVH = 8
HD = 128
DV = 8192
MAXT = 4
VTOK = 16
LEN = 128
IMG_DEV = 8
SEQ_DEV = 12
PICKS = 2
CAP = 2
IMAGES = 128
SEQS = 192
KEYS_IMG = 64
TEXT_TOK = 24576
N_TXT = 16


def draw_image_ids(key, part):
    key = jax.random.fold_in(key, 11)
    request_total = SEQ_DEV * PICKS
    shard_keys = jax.random.split(key, N_TXT)

    def one_shard(sub_key):
        perm_key, inner_key = jax.random.split(sub_key)
        chosen = jax.random.permutation(perm_key, CAP * N_TXT)[:request_total]
        owner_shard = chosen // CAP
        inner = jax.random.randint(inner_key, (request_total,), 0, IMG_DEV)
        return (owner_shard * IMG_DEV + inner).astype(jnp.int32)
    return jax.vmap(one_shard)(shard_keys).reshape(SEQS, PICKS)


def draw_tile_count(key, part):
    key = jax.random.fold_in(key, 23)
    base_key, high_key, step_key = jax.random.split(key, 3)
    counts = jax.random.randint(base_key, (IMAGES,), 1, MAXT + 1)
    high_at = jax.random.randint(high_key, (), 0, IMAGES)
    low_at = (high_at + 1 + jax.random.randint(step_key, (), 0, IMAGES - 1)) % IMAGES
    counts = counts.at[high_at].set(MAXT).at[low_at].set(1)
    return counts.astype(jnp.int32)


def draw_text_len(key, part):
    key = jax.random.fold_in(key, 37)
    base_key, high_key, step_key = jax.random.split(key, 3)
    lengths = jax.random.randint(base_key, (SEQS,), LEN // 8, LEN + 1)
    high_at = jax.random.randint(high_key, (), 0, SEQS)
    low_at = (high_at + 1 + jax.random.randint(step_key, (), 0, SEQS - 1)) % SEQS
    lengths = lengths.at[high_at].set(LEN).at[low_at].set(LEN // 8)
    return lengths.astype(jnp.int32)


def draw_queries(key, part):
    key = jax.random.fold_in(key, 41)
    base_key = jax.random.fold_in(key, 0)
    values = jax.random.truncated_normal(base_key, -6.0, 6.0, (TEXT_TOK, HEADS * HD), jnp.float32)
    return values.astype(jnp.bfloat16)


def steps_of(stream_key, dims, cuts, smallest, high):
    def one(axis_at, parts):
        steps = jax.random.uniform(jax.random.fold_in(jax.random.fold_in(stream_key, 6), axis_at), (parts,), jnp.float32, smallest / len(cuts), high / len(cuts))
        return jnp.repeat(jnp.exp(steps), dims[axis_at] // parts).reshape((-1,) + (1,) * (len(dims) - axis_at - 1))

    level = one(*cuts[0])
    for cut in cuts[1:]:
        level = level * one(*cut)
    return level


def normal_values(key, shape, spread, limit, pieces=(), dtype=jnp.bfloat16):
    entries = spread * jax.random.normal(key, shape, jnp.float32)
    if pieces:
        entries = entries * steps_of(key, shape, pieces, -0.22, 0.18)
    return jnp.clip(entries, -limit, limit).astype(dtype)


def setup_inputs(seed: int = 0) -> dict:
    seeds = jax.random.split(jax.random.key(seed), 8)
    features = normal_values(seeds[0], (IMAGES, KEYS_IMG, DV), 1.0, 6.0, ((0, 16),))
    tile_count = draw_tile_count(jax.random.fold_in(seeds[7], 71), 0)
    kv_weight = normal_values(seeds[2], (DV, 2, KVH * HD), DV ** -0.5, 0.0625, ((2, 8),))
    queries = draw_queries(jax.random.fold_in(seeds[7], 71), 0)
    out_grad = normal_values(seeds[4], (TEXT_TOK, HEADS * HD), 1.0, 6.0, ((0, 16), (1, 8)))
    image_ids = draw_image_ids(jax.random.fold_in(seeds[7], 71), 0)
    text_len = draw_text_len(jax.random.fold_in(seeds[7], 71), 0)
    return dict(features=features, tile_count=tile_count, kv_weight=kv_weight, queries=queries, out_grad=out_grad, image_ids=image_ids, text_len=text_len)


def attend_seq(query_blk, pair_blk, key_live, row_live, grad_blk):
    inv_root = 1.0 / math.sqrt(query_blk.shape[-1])
    query_wide = query_blk.astype(jnp.float32)
    keys_wide = pair_blk[:, 0].astype(jnp.float32)
    vals_wide = pair_blk[:, 1].astype(jnp.float32)
    scores = jnp.einsum('lhgd,khd->hglk', query_wide, keys_wide) * inv_root
    scores = jnp.where(key_live[None, None, None, :], scores, -jnp.inf)
    top_score = lax.optimization_barrier(jnp.max(scores, axis=-1, keepdims=True))
    expo = jnp.exp(scores - top_score)
    probs = expo / lax.optimization_barrier(jnp.sum(expo, axis=-1, keepdims=True))
    probs_low = lax.optimization_barrier(probs.astype(jnp.bfloat16)).astype(jnp.float32)
    attended = jnp.einsum('hglk,khd->lhgd', probs_low, vals_wide)
    row_mask = row_live[:, None, None, None]
    attended = jnp.where(row_mask, attended, 0.0)
    grad_live = jnp.where(row_mask, grad_blk.astype(jnp.float32), 0.0)
    delta_sum = lax.optimization_barrier(jnp.sum(grad_live * attended, axis=-1))
    grad_probs = jnp.einsum('lhgd,khd->hglk', grad_live, vals_wide)
    grad_scores = probs * (grad_probs - jnp.transpose(delta_sum, (1, 2, 0))[..., None])
    scores_low = lax.optimization_barrier(grad_scores.astype(jnp.bfloat16)).astype(jnp.float32)
    grad_query = jnp.einsum('hglk,khd->lhgd', scores_low, keys_wide) * inv_root
    grad_keys = jnp.einsum('hglk,lhgd->khd', scores_low, query_wide) * inv_root
    grad_vals = jnp.einsum('hglk,lhgd->khd', probs_low, grad_live)
    pair_grad = jnp.stack([grad_keys, grad_vals], axis=1).astype(jnp.bfloat16)
    return (attended.astype(jnp.bfloat16), grad_query.astype(jnp.bfloat16), pair_grad)

def reference(features, tile_count, kv_weight, queries, out_grad, image_ids, text_len):
    group_size = HEADS // KVH
    flat_weight = kv_weight.reshape(DV, 2 * KVH * HD)
    keyval = lax.map(lambda rows: jnp.dot(rows, flat_weight, preferred_element_type=jnp.float32).astype(jnp.bfloat16), features)
    key_tile = jnp.arange(KEYS_IMG) // VTOK
    query_seq = queries.reshape(SEQS, LEN, KVH, group_size, HD)
    grad_seq = out_grad.reshape(SEQS, LEN, KVH, group_size, HD)

    def per_seq(accum, inputs):
        query_blk, grad_blk, seq_ids, seq_len = inputs
        pair_rows = jnp.take(keyval, seq_ids, axis=0).reshape(PICKS * KEYS_IMG, 2, KVH, HD)
        counts = jnp.take(tile_count, seq_ids, axis=0)
        key_live = (key_tile[None, :] < counts[:, None]).reshape(PICKS * KEYS_IMG)
        row_live = jnp.arange(LEN) < seq_len
        attended, grad_query, pair_grad = attend_seq(query_blk, pair_rows, key_live, row_live, grad_blk)
        pair_flat = pair_grad.reshape(PICKS, KEYS_IMG, 2 * KVH * HD).astype(jnp.float32)
        accum = accum.at[seq_ids].add(pair_flat)
        return (accum, (attended, grad_query))
    start = jnp.zeros((IMAGES, KEYS_IMG, 2 * KVH * HD), jnp.float32)
    accum, (attended, grad_query) = lax.scan(per_seq, start, (query_seq, grad_seq, image_ids.astype(jnp.int32), text_len))

    def per_image(total, inputs):
        rows, grads = inputs
        part_sum = jnp.dot(rows.astype(jnp.float32).T, grads, precision=lax.Precision.HIGHEST)
        return (total + part_sum, None)
    weight_grad, _ = lax.scan(per_image, jnp.zeros((DV, 2 * KVH * HD), jnp.float32), (features, accum))
    attn_out = attended.reshape(TEXT_TOK, HEADS * HD)
    query_grad = grad_query.reshape(TEXT_TOK, HEADS * HD)
    return (attn_out, query_grad, weight_grad.reshape(DV, 2, KVH * HD))
```

```python
import functools
import math

import jax
import jax.numpy as jnp
from jax import lax
from jax.experimental import pallas as pl
from jax.experimental.pallas import tpu as pltpu
from jax.sharding import PartitionSpec as P

HD = 128
MAXT = 4
SIDE = 4
CAP = 2
BF16 = jnp.bfloat16
F32 = jnp.float32
VMEM_LIMIT = 48 * 1024 * 1024


def request_order(flat_ids, img_dev):
    shard_of = flat_ids // img_dev
    total = flat_ids.shape[0]
    same_shard = shard_of[:, None] == shard_of[None, :]
    earlier = jnp.arange(total)[None, :] < jnp.arange(total)[:, None]
    position = jnp.sum(jnp.logical_and(same_shard, earlier).astype(jnp.int32), axis=1)
    return shard_of, position


def fill_kernel(table, pairs, slots):
    for slot in range(slots.shape[0]):
        image = jnp.maximum(table[slot // CAP, slot % CAP] - 1, 0)
        slots[slot] = pairs[image]


def attend_kernel(meta, table, queries, grads, slots, attn, query_grad, slot_grad, *, seq_dev, img_dev):
    seq = pl.program_id(0)
    seq_len = queries.shape[0]
    groups = queries.shape[1] // HD
    keys_img = slots.shape[1]
    inv_root = 1.0 / math.sqrt(HD)
    scale = inv_root * math.log2(math.e)

    @pl.when(seq == 0)
    def _():
        slot_grad[...] = jnp.zeros_like(slot_grad)

    text_len = meta[4 * seq_dev + seq]
    slot_ids = [meta[2 * seq + pick] for pick in range(2)]
    images = [meta[2 * seq_dev + 2 * seq + pick] for pick in range(2)]
    tiles = [table[image // img_dev, 8 + image % img_dev] for image in images]
    pair = [slots[slot] for slot in slot_ids]
    keys = jnp.concatenate([blk[:, :HD] for blk in pair], axis=0)
    vals = jnp.concatenate([blk[:, HD:] for blk in pair], axis=0)
    none = jnp.zeros_like(keys)
    key_val = jnp.concatenate(
        [jnp.concatenate([keys, none], axis=1), jnp.concatenate([none, vals], axis=1)], axis=0
    )
    val_key = jnp.concatenate(
        [jnp.concatenate([vals, none], axis=1), jnp.concatenate([none, keys], axis=1)], axis=0
    )
    column = lax.broadcasted_iota(jnp.int32, (1, 2 * keys_img), 1)
    tile_rows = keys_img // MAXT
    live_to = jnp.where(
        column < keys_img, tiles[0] * tile_rows, keys_img + tiles[1] * tile_rows
    )
    bias = jnp.where(column < live_to, 0.0, -jnp.inf).astype(F32)
    row = lax.broadcasted_iota(jnp.int32, (groups, seq_len, 1), 1).reshape(groups * seq_len, 1)
    row_live = row < text_len

    both = jnp.concatenate(
        [
            jnp.concatenate(
                [queries[:, h * HD : (h + 1) * HD], grads[:, h * HD : (h + 1) * HD]], axis=1
            )
            for h in range(groups)
        ],
        axis=0,
    )
    wide = lax.dot_general(both, key_val, (((1,), (1,)), ((), ())), preferred_element_type=F32)
    scores = wide[:, :HD] + bias
    grad_probs = wide[:, HD:]
    top = jnp.max(scores, axis=1, keepdims=True)
    expo = jnp.exp2((scores - top) * scale)
    inverse = jnp.where(row_live, 1.0 / jnp.sum(expo, axis=1, keepdims=True), 0.0)
    probs = expo * inverse
    probs_low = probs.astype(BF16)
    delta = jnp.sum(probs_low.astype(F32) * grad_probs, axis=1, keepdims=True)
    scores_low = (probs * (grad_probs - delta)).astype(BF16)
    low = jnp.concatenate([probs_low, scores_low], axis=1)
    result = jnp.dot(low, val_key, preferred_element_type=F32)
    for h in range(groups):
        rows = slice(h * seq_len, (h + 1) * seq_len)
        cols = slice(h * HD, (h + 1) * HD)
        attn[:, cols] = result[rows, :HD].astype(BF16)
        query_grad[:, cols] = (result[rows, HD:] * inv_root).astype(BF16)
    back = lax.dot_general(low, both, (((0,), (0,)), ((), ())), preferred_element_type=F32)
    val_grad = back[:HD, HD:].astype(BF16)
    key_grad = (back[HD:, :HD] * inv_root).astype(BF16)
    for pick in range(2):
        rows = slice(pick * keys_img, (pick + 1) * keys_img)
        slot_grad[slot_ids[pick]] = jnp.concatenate([key_grad[rows], val_grad[rows]], axis=1)


def weight_kernel(table, place, slot_grad, features, *rest, img_dev):
    outs = rest[:10]
    image_grad, rows, sems = rest[10:]
    slot_total, keys_img, cols = slot_grad.shape
    block = rows.shape[2]
    x_at, z_at = place[0], place[1]
    order = [2, 1, 3, 0]
    steps = sorted(
        [(dx, dz) for dx in range(SIDE) for dz in range(SIDE)],
        key=lambda d: min(order.index(d[0]), order.index(d[1])),
    )

    def fetch(step):
        dx, dz = steps[step]
        dest = lax.rem(x_at + dx, SIDE) * SIDE + lax.rem(z_at + dz, SIDE)
        start = pl.multiple_of(dest * block, block)
        return pltpu.make_async_copy(
            features.at[:, pl.ds(start, block)], rows.at[step], sems.at[step]
        )

    for step in range(len(steps)):
        fetch(step).start()
    image_grad[...] = jnp.zeros_like(image_grad)
    for slot in range(slot_total):
        image = table[slot // CAP, slot % CAP]

        @pl.when(image > 0)
        def _():
            image_grad[image - 1] += slot_grad[slot].astype(F32)

    grad_low = image_grad[...].reshape(img_dev * keys_img, cols).astype(BF16)
    for step, (dx, dz) in enumerate(steps):
        fetch(step).wait()
        part = lax.dot_general(
            grad_low, rows[step], (((0,), (0,)), ((), ())), preferred_element_type=F32
        ).astype(BF16)
        for half, (first, second) in enumerate(((dx, dz), (dz, dx))):
            piece = part[half * HD : (half + 1) * HD]
            five = outs[5 * half : 5 * half + 5]
            if first == 0:
                five[4][second] = piece
            elif first == 1:
                five[0][second] = piece
            elif first == 3:
                five[1][second] = piece
            elif second < 2:
                five[2][second] = piece
            else:
                five[3][second - 2] = piece


def final_kernel(*refs):
    out = refs[-1]
    for half in range(2):
        own, one, two, three = refs[4 * half : 4 * half + 4]
        total = own[...] + one[...].astype(F32) + two[...].astype(F32) + three[...].astype(F32)
        out[:, half, :] = total.T


def shift(values, axis, step):
    pairs = []
    for x in range(SIDE):
        for z in range(SIDE):
            to = ((x + step) % SIDE, z) if axis == "x" else (x, (z + step) % SIDE)
            pairs.append((x * SIDE + z, to[0] * SIDE + to[1]))
    return lax.ppermute(values, "txt", pairs)


def add(*terms):
    return functools.reduce(lambda a, b: a + b, [term.astype(F32) for term in terms])


def shards(features, tile_count, kv_weight, queries, out_grad, image_ids, text_len):
    txt_count = lax.axis_size("txt")
    shard_index = lax.axis_index("txt")
    img_dev, keys_img, feat_width = features.shape
    seq_dev, picks = image_ids.shape
    head_cols = kv_weight.shape[2]
    cols = 2 * head_cols
    request_total = seq_dev * picks
    slot_total = txt_count * CAP
    seq_len = queries.shape[0] // seq_dev
    whole = pl.BlockSpec(memory_space=pltpu.VMEM)
    scalars = pl.BlockSpec(memory_space=pltpu.SMEM)
    params = pltpu.CompilerParams(vmem_limit_bytes=VMEM_LIMIT)

    flat_ids = image_ids.reshape(request_total)
    own_shard, own_position = request_order(flat_ids, img_dev)
    flat_index = own_shard * CAP + own_position
    lane = jnp.arange(128)
    wanted = jnp.sum(
        jnp.where(
            flat_index[None, None, :]
            == jnp.arange(txt_count)[:, None, None] * CAP + lane[None, :, None],
            jnp.where(lane[None, :, None] < CAP, flat_ids % img_dev + 1, 0),
            0,
        ),
        axis=-1,
    )
    counts = jnp.pad(tile_count, (8, 128 - 8 - img_dev))
    table = lax.all_to_all(wanted + counts[None, :], "txt", 0, 0, tiled=True)
    meta = jnp.concatenate([flat_index, flat_ids, text_len])
    place = jnp.stack([shard_index // SIDE, shard_index % SIDE])

    flat_features = features.reshape(img_dev * keys_img, feat_width)
    own_pairs = jnp.dot(
        flat_features, kv_weight.reshape(feat_width, cols), preferred_element_type=F32
    ).astype(BF16)
    sent_pairs = pl.pallas_call(
        fill_kernel,
        out_shape=jax.ShapeDtypeStruct((slot_total, keys_img, cols), BF16),
        in_specs=[scalars, whole],
        out_specs=whole,
        compiler_params=params,
        name="fill_slots",
    )(table, own_pairs.reshape(img_dev, keys_img, cols))
    got_pairs = lax.all_to_all(
        sent_pairs.reshape(txt_count, CAP, keys_img, cols), "txt", 0, 0, tiled=True
    ).reshape(slot_total, keys_img, cols)

    token_block = pl.BlockSpec((seq_len, queries.shape[1]), lambda s, *_: (s, 0))
    slot_block = pl.BlockSpec((slot_total, keys_img, cols), lambda s, *_: (0, 0, 0))
    attended, grad_query, slot_grad = pl.pallas_call(
        functools.partial(attend_kernel, seq_dev=seq_dev, img_dev=img_dev),
        out_shape=[
            jax.ShapeDtypeStruct(queries.shape, BF16),
            jax.ShapeDtypeStruct(queries.shape, BF16),
            jax.ShapeDtypeStruct((slot_total, keys_img, cols), BF16),
        ],
        grid_spec=pltpu.PrefetchScalarGridSpec(
            num_scalar_prefetch=2,
            grid=(seq_dev,),
            in_specs=[token_block, token_block, slot_block],
            out_specs=[token_block, token_block, slot_block],
        ),
        compiler_params=params,
        name="attend",
    )(meta, table, queries, out_grad, got_pairs)

    back_grad = lax.all_to_all(
        slot_grad.reshape(txt_count, CAP, keys_img, cols), "txt", 0, 0, tiled=True
    ).reshape(slot_total, keys_img, cols)

    block = feat_width // txt_count
    message = [(SIDE, HD, block), (SIDE, HD, block), (2, HD, block), (2, HD, block), (SIDE, HD, block)]
    pieces = pl.pallas_call(
        functools.partial(weight_kernel, img_dev=img_dev),
        out_shape=[jax.ShapeDtypeStruct(shape, BF16) for shape in message * 2],
        in_specs=[scalars, scalars, whole, pl.BlockSpec(memory_space=pl.ANY)],
        out_specs=[whole] * 10,
        scratch_shapes=[
            pltpu.VMEM((img_dev, keys_img, cols), F32),
            pltpu.VMEM((txt_count, img_dev * keys_img, block), BF16),
            pltpu.SemaphoreType.DMA((txt_count,)),
        ],
        compiler_params=params,
        name="weight_part",
    )(table, place, back_grad, flat_features)

    final = []
    for half, (first, second) in enumerate((("x", "z"), ("z", "x"))):
        up, down, far_low, far_high, own = pieces[5 * half : 5 * half + 5]
        far_up = shift(far_low, first, 1)
        far_down = shift(far_high, first, -1)
        near_up = shift(up[2:], first, 1)
        near_down = shift(down[:2], first, -1)
        relay_up = shift(add(up[:2], far_up).astype(BF16), first, 1)
        relay_down = shift(add(down[2:], far_down).astype(BF16), first, -1)
        low = add(own[:2], relay_up, near_down)
        high = add(own[2:], near_up, relay_down)
        final += [
            low[0],
            shift(low[1].astype(BF16), second, 1),
            shift(high[0].astype(BF16), second, 2),
            shift(high[1].astype(BF16), second, -1),
        ]
    weight_grad = pl.pallas_call(
        final_kernel,
        out_shape=jax.ShapeDtypeStruct((block, 2, head_cols), F32),
        in_specs=[whole] * 8,
        out_specs=whole,
        compiler_params=params,
        name="weight_total",
    )(*final)
    return attended, grad_query, weight_grad


def solution(mesh):
    in_specs = (
        P("txt", None, None),
        P("txt"),
        P(None, None, "img"),
        P("txt", "img"),
        P("txt", "img"),
        P("txt", None),
        P("txt"),
    )
    out_specs = (P("txt", "img"), P("txt", "img"), P("txt", None, "img"))
    return jax.shard_map(shards, mesh=mesh, in_specs=in_specs, out_specs=out_specs, check_vma=False)
```

```python
import functools
import math

import jax
import jax.numpy as jnp
from jax import lax
from jax.experimental import pallas as pl
from jax.experimental.pallas import tpu as pltpu
from jax.sharding import PartitionSpec as P

HD = 128
MAXT = 4
SIDE = 4
CAP = 2
BF16 = jnp.bfloat16
F32 = jnp.float32
MIB = 1024 * 1024


def request_kernel(ids, counts, table, meta, seen, *, img_dev):
    shards, lanes = table.shape
    picks, seq_dev = ids.shape
    for shard in range(shards):
        seen[shard] = 0
    row = lax.broadcasted_iota(jnp.int32, (shards, lanes), 0)
    lane = lax.broadcasted_iota(jnp.int32, (shards, lanes), 1)
    value = jnp.zeros((shards, lanes), jnp.int32)
    for image in range(img_dev):
        value = jnp.where(lane == 8 + image, counts[image], value)
    for request in range(picks * seq_dev):
        image = ids[request % picks, request // picks]
        shard = image // img_dev
        position = seen[shard]
        seen[shard] = position + 1
        value = jnp.where(
            jnp.logical_and(row == shard, lane == position), image % img_dev + 1, value
        )
        meta[request] = shard * CAP + position
        meta[picks * seq_dev + request] = image
    table[...] = value


def fill_kernel(table, pairs, slots):
    for slot in range(slots.shape[0]):
        image = jnp.maximum(table[slot // CAP, slot % CAP] - 1, 0)
        slots[slot] = pairs[image]


def attend_kernel(meta, table, lengths, queries, grads, slots, attn, query_grad, slot_grad, *scratch, img_dev):
    q_all, g_all, out_all, dq_all, sems = scratch
    seq_dev = lengths.shape[0]
    seq_len = queries.shape[0] // seq_dev
    groups = queries.shape[1] // HD
    keys_img = slots.shape[1]
    inv_root = 1.0 / math.sqrt(HD)
    scale = inv_root * math.log2(math.e)
    unroll = 6

    def rows_of(seq):
        return pl.ds(pl.multiple_of(seq * seq_len, seq_len), seq_len)

    ends = ((queries, q_all), (grads, g_all), (out_all, attn), (dq_all, query_grad))

    def copies(seq, kinds):
        rows = rows_of(seq)
        return [
            pltpu.make_async_copy(
                ends[kind][0].at[rows], ends[kind][1].at[rows], sems.at[kind, seq]
            )
            for kind in kinds
        ]

    def begin(seq):
        for copy in copies(seq, (0, 1)):
            copy.wait()
        slot_ids = [meta[2 * seq + pick] for pick in range(2)]
        images = [meta[2 * seq_dev + 2 * seq + pick] for pick in range(2)]
        tiles = [table[image // img_dev, 8 + image % img_dev] for image in images]
        pair = [slots[slot] for slot in slot_ids]
        keys = jnp.concatenate([blk[:, :HD] for blk in pair], axis=0)
        vals = jnp.concatenate([blk[:, HD:] for blk in pair], axis=0)
        none = jnp.zeros_like(keys)
        key_val = jnp.concatenate(
            [jnp.concatenate([keys, none], axis=1), jnp.concatenate([none, vals], axis=1)], axis=0
        )
        val_key = jnp.concatenate(
            [jnp.concatenate([vals, none], axis=1), jnp.concatenate([none, keys], axis=1)], axis=0
        )
        key = lax.broadcasted_iota(jnp.int32, (2 * keys_img, 1), 0)
        tile_rows = keys_img // MAXT
        live_to = jnp.where(key < keys_img, tiles[0] * tile_rows, keys_img + tiles[1] * tile_rows)
        bias = jnp.where(key < live_to, 0.0, -jnp.inf).astype(F32)
        rows = rows_of(seq)
        both = jnp.concatenate(
            [
                jnp.concatenate(
                    [q_all[rows, h * HD : (h + 1) * HD], g_all[rows, h * HD : (h + 1) * HD]], axis=1
                )
                for h in range(groups)
            ],
            axis=0,
        )
        wide = lax.dot_general(key_val, both, (((1,), (1,)), ((), ())), preferred_element_type=F32)
        return slot_ids, val_key, both, wide[: 2 * keys_img] + bias, wide[2 * keys_img :]

    def finish(seq, state):
        slot_ids, val_key, both, scores, grad_probs = state
        token = lax.broadcasted_iota(jnp.int32, (1, groups * seq_len), 1)
        live = token % seq_len < lengths[seq]
        top = jnp.max(scores, axis=0, keepdims=True)
        expo = jnp.exp2((scores - top) * scale)
        probs = expo * jnp.where(live, 1.0 / jnp.sum(expo, axis=0, keepdims=True), 0.0)
        probs_low = probs.astype(BF16)
        delta = jnp.sum(probs_low.astype(F32) * grad_probs, axis=0, keepdims=True)
        scores_low = (probs * (grad_probs - delta)).astype(BF16)
        low = jnp.concatenate([probs_low, scores_low], axis=0)
        back = jnp.dot(low, both, preferred_element_type=F32)
        result = lax.dot_general(low, val_key, (((0,), (0,)), ((), ())), preferred_element_type=F32)
        rows = rows_of(seq)
        for h in range(groups):
            part = result[h * seq_len : (h + 1) * seq_len]
            out_all[rows, h * HD : (h + 1) * HD] = part[:, :HD].astype(BF16)
            dq_all[rows, h * HD : (h + 1) * HD] = (part[:, HD:] * inv_root).astype(BF16)
        for copy in copies(seq, (2, 3)):
            copy.start()
        val_grad = back[: 2 * keys_img, HD:].astype(BF16)
        key_grad = (back[2 * keys_img :, :HD] * inv_root).astype(BF16)
        for pick in range(2):
            part = slice(pick * keys_img, (pick + 1) * keys_img)
            slot_grad[slot_ids[pick]] = jnp.concatenate([key_grad[part], val_grad[part]], axis=1)

    for seq in range(seq_dev):
        for copy in copies(seq, (0, 1)):
            copy.start()

    @pl.loop(0, seq_dev // unroll)
    def _(turn):
        state = begin(turn * unroll)
        for step in range(unroll):
            seq = turn * unroll + step
            after = begin(seq + 1) if step + 1 < unroll else None
            finish(seq, state)
            state = after

    for seq in range(seq_dev):
        for copy in copies(seq, (2, 3)):
            copy.wait()


def weight_kernel(table, place, slot_grad, features, *rest, img_dev):
    outs = rest[:10]
    image_grad, grad_low, rows, sems = rest[10:]
    slot_total, keys_img, cols = slot_grad.shape
    block = outs[0].shape[2]
    x_at, z_at = place[0], place[1]
    order = (2, 1, 3, 0)

    def fetch(dx):
        start = pl.multiple_of(lax.rem(x_at + dx, SIDE) * (SIDE * block), SIDE * block)
        return pltpu.make_async_copy(
            features.at[:, pl.ds(start, SIDE * block)], rows.at[dx], sems.at[dx]
        )

    for dx in order:
        fetch(dx).start()
    image_grad[...] = jnp.zeros_like(image_grad)
    for slot in range(slot_total):
        image = table[slot // CAP, slot % CAP]

        @pl.when(image > 0)
        def _():
            image_grad[image - 1] += slot_grad[slot].astype(F32)

    grad_low[...] = image_grad[...].reshape(img_dev * keys_img, cols).T.astype(BF16)
    for dx in order:
        fetch(dx).wait()
        for dz in range(SIDE):
            start = pl.multiple_of(lax.rem(z_at + dz, SIDE) * block, block)
            part = jnp.dot(
                grad_low[...], rows[dx, :, pl.ds(start, block)], preferred_element_type=F32
            ).astype(BF16)
            for half, (first, second) in enumerate(((dx, dz), (dz, dx))):
                piece = part[half * HD : (half + 1) * HD]
                five = outs[5 * half : 5 * half + 5]
                if first == 0:
                    five[4][second] = piece
                elif first == 1:
                    five[0][second] = piece
                elif first == 3:
                    five[1][second] = piece
                elif second < 2:
                    five[2][second] = piece
                else:
                    five[3][second - 2] = piece


def final_kernel(*refs):
    out = refs[-1]
    for half in range(2):
        own, one, two, three = refs[4 * half : 4 * half + 4]
        total = own[...] + one[...].astype(F32) + two[...].astype(F32) + three[...].astype(F32)
        out[:, half, :] = total.T


def shift(values, axis, step):
    pairs = []
    for x in range(SIDE):
        for z in range(SIDE):
            to = ((x + step) % SIDE, z) if axis == "x" else (x, (z + step) % SIDE)
            pairs.append((x * SIDE + z, to[0] * SIDE + to[1]))
    return lax.ppermute(values, "txt", pairs)


def add(*terms):
    return functools.reduce(lambda a, b: a + b, [term.astype(F32) for term in terms])


def shards(features, tile_count, kv_weight, queries, out_grad, image_ids, text_len):
    txt_count = lax.axis_size("txt")
    shard_index = lax.axis_index("txt")
    img_dev, keys_img, feat_width = features.shape
    seq_dev, picks = image_ids.shape
    head_cols = kv_weight.shape[2]
    cols = 2 * head_cols
    request_total = seq_dev * picks
    slot_total = txt_count * CAP
    whole = pl.BlockSpec(memory_space=pltpu.VMEM)
    scalars = pl.BlockSpec(memory_space=pltpu.SMEM)

    def params(mib):
        return pltpu.CompilerParams(vmem_limit_bytes=mib * MIB)


    wanted, meta = pl.pallas_call(
        functools.partial(request_kernel, img_dev=img_dev),
        out_shape=[
            jax.ShapeDtypeStruct((txt_count, 128), jnp.int32),
            jax.ShapeDtypeStruct((2 * request_total,), jnp.int32),
        ],
        in_specs=[scalars, scalars],
        out_specs=[whole, scalars],
        scratch_shapes=[pltpu.SMEM((txt_count,), jnp.int32)],
        name="request_table",
    )(image_ids.T, tile_count)
    table = lax.all_to_all(wanted, "txt", 0, 0, tiled=True)
    place = jnp.stack([shard_index // SIDE, shard_index % SIDE])

    flat_features = features.reshape(img_dev * keys_img, feat_width)
    own_pairs = jnp.dot(
        flat_features, kv_weight.reshape(feat_width, cols), preferred_element_type=F32
    ).astype(BF16)
    sent_pairs = pl.pallas_call(
        fill_kernel,
        out_shape=jax.ShapeDtypeStruct((slot_total, keys_img, cols), BF16),
        in_specs=[scalars, whole],
        out_specs=whole,
        compiler_params=params(8),
        name="fill_slots",
    )(table, own_pairs.reshape(img_dev, keys_img, cols))
    got_pairs = lax.all_to_all(
        sent_pairs.reshape(txt_count, CAP, keys_img, cols), "txt", 0, 0, tiled=True
    ).reshape(slot_total, keys_img, cols)

    in_hbm = pl.BlockSpec(memory_space=pltpu.HBM)
    attended, grad_query, slot_grad = pl.pallas_call(
        functools.partial(attend_kernel, img_dev=img_dev),
        out_shape=[
            jax.ShapeDtypeStruct(queries.shape, BF16),
            jax.ShapeDtypeStruct(queries.shape, BF16),
            jax.ShapeDtypeStruct((slot_total, keys_img, cols), BF16),
        ],
        in_specs=[scalars, scalars, scalars, in_hbm, in_hbm, whole],
        out_specs=[in_hbm, in_hbm, whole],
        scratch_shapes=[pltpu.VMEM(queries.shape, BF16)] * 4
        + [pltpu.SemaphoreType.DMA((4, seq_dev))],
        compiler_params=params(24),
        name="attend",
    )(meta, table, text_len, *[pltpu.with_memory_space_constraint(x, pltpu.HBM) for x in (queries, out_grad)], got_pairs)
    back_grad = lax.all_to_all(
        slot_grad.reshape(txt_count, CAP, keys_img, cols), "txt", 0, 0, tiled=True
    ).reshape(slot_total, keys_img, cols)

    block = feat_width // txt_count
    message = [(SIDE, HD, block), (SIDE, HD, block), (2, HD, block), (2, HD, block), (SIDE, HD, block)]
    pieces = pl.pallas_call(
        functools.partial(weight_kernel, img_dev=img_dev),
        out_shape=[jax.ShapeDtypeStruct(shape, BF16) for shape in message * 2],
        in_specs=[scalars, scalars, whole, in_hbm],
        out_specs=[whole] * 10,
        scratch_shapes=[
            pltpu.VMEM((img_dev, keys_img, cols), F32),
            pltpu.VMEM((cols, img_dev * keys_img), BF16),
            pltpu.VMEM((SIDE, img_dev * keys_img, SIDE * block), BF16),
            pltpu.SemaphoreType.DMA((SIDE,)),
        ],
        compiler_params=params(20),
        name="weight_part",
    )(table, place, back_grad, pltpu.with_memory_space_constraint(flat_features, pltpu.HBM))

    final = []
    for half, (first, second) in enumerate((("x", "z"), ("z", "x"))):
        up, down, far_low, far_high, own = pieces[5 * half : 5 * half + 5]
        far_up = shift(far_low, first, 1)
        far_down = shift(far_high, first, -1)
        near_up = shift(up[2:], first, 1)
        near_down = shift(down[:2], first, -1)
        relay_up = shift(add(up[:2], far_up).astype(BF16), first, 1)
        relay_down = shift(add(down[2:], far_down).astype(BF16), first, -1)
        low = add(own[:2], relay_up, near_down)
        high = add(own[2:], near_up, relay_down)
        final += [
            low[0],
            shift(low[1].astype(BF16), second, 1),
            shift(high[0].astype(BF16), second, 2),
            shift(high[1].astype(BF16), second, -1),
        ]
    weight_grad = pl.pallas_call(
        final_kernel,
        out_shape=jax.ShapeDtypeStruct((block, 2, head_cols), F32),
        in_specs=[whole] * 8,
        out_specs=whole,
        compiler_params=params(8),
        name="weight_total",
    )(*final)
    return attended, grad_query, weight_grad


def solution(mesh):
    in_specs = (
        P("txt", None, None),
        P("txt"),
        P(None, None, "img"),
        P("txt", "img"),
        P("txt", "img"),
        P("txt", None),
        P("txt"),
    )
    out_specs = (P("txt", "img"), P("txt", "img"), P("txt", None, "img"))
    return jax.shard_map(shards, mesh=mesh, in_specs=in_specs, out_specs=out_specs, check_vma=False)
```

```python
import functools
import math

import jax
import jax.numpy as jnp
from jax import lax
from jax.experimental import pallas as pl
from jax.experimental.pallas import tpu as pltpu
from jax.sharding import PartitionSpec as P

HD = 128
MAXT = 4
SIDE = 4
CAP = 2
BF16 = jnp.bfloat16
F32 = jnp.float32
MIB = 1024 * 1024


def request_kernel(ids, counts, table, meta, seen, *, img_dev):
    shards, lanes = table.shape
    picks, seq_dev = ids.shape
    for shard in range(shards):
        seen[shard] = 0
    row = lax.broadcasted_iota(jnp.int32, (shards, lanes), 0)
    lane = lax.broadcasted_iota(jnp.int32, (shards, lanes), 1)
    value = jnp.zeros((shards, lanes), jnp.int32)
    for image in range(img_dev):
        value = jnp.where(lane == 8 + image, counts[image], value)
    for request in range(picks * seq_dev):
        image = ids[request % picks, request // picks]
        shard = image // img_dev
        position = seen[shard]
        seen[shard] = position + 1
        value = jnp.where(
            jnp.logical_and(row == shard, lane == position), image % img_dev + 1, value
        )
        meta[request] = shard * CAP + position
        meta[picks * seq_dev + request] = image
    table[...] = value


def fill_kernel(table, pairs, slots, sems):
    copies = []
    for slot in range(slots.shape[0]):
        image = jnp.maximum(table[slot // CAP, slot % CAP] - 1, 0)
        copies.append(pltpu.make_async_copy(pairs.at[image], slots.at[slot], sems.at[slot]))
    for copy in copies:
        copy.start()
    for copy in copies:
        copy.wait()


def attend_kernel(meta, table, lengths, queries, grads, slots, attn, query_grad, slot_grad, *scratch, img_dev):
    q_all, g_all, out_all, dq_all, pair_grad, sems, pair_sems = scratch
    seq_dev = lengths.shape[0]
    seq_len = queries.shape[0] // seq_dev
    groups = queries.shape[1] // HD
    keys_img = slots.shape[1]
    inv_root = 1.0 / math.sqrt(HD)
    scale = inv_root * math.log2(math.e)
    unroll = 6

    def rows_of(seq):
        return pl.ds(pl.multiple_of(seq * seq_len, seq_len), seq_len)

    ends = ((queries, q_all), (grads, g_all), (out_all, attn), (dq_all, query_grad))

    def copies(seq, kinds):
        rows = rows_of(seq)
        return [
            pltpu.make_async_copy(
                ends[kind][0].at[rows], ends[kind][1].at[rows], sems.at[kind, seq]
            )
            for kind in kinds
        ]

    def pair_copy(seq, pick):
        at = 2 * seq + pick
        return pltpu.make_async_copy(
            pair_grad.at[at], slot_grad.at[meta[at]], pair_sems.at[at]
        )

    def begin(seq):
        for copy in copies(seq, (0, 1)):
            copy.wait()
        slot_ids = [meta[2 * seq + pick] for pick in range(2)]
        images = [meta[2 * seq_dev + 2 * seq + pick] for pick in range(2)]
        tiles = [table[image // img_dev, 8 + image % img_dev] for image in images]
        pair = [slots[slot] for slot in slot_ids]
        keys = jnp.concatenate([blk[:, :HD] for blk in pair], axis=0)
        vals = jnp.concatenate([blk[:, HD:] for blk in pair], axis=0)
        none = jnp.zeros_like(keys)
        key_val = jnp.concatenate(
            [jnp.concatenate([keys, none], axis=1), jnp.concatenate([none, vals], axis=1)], axis=0
        )
        val_key = jnp.concatenate(
            [jnp.concatenate([vals, none], axis=1), jnp.concatenate([none, keys], axis=1)], axis=0
        )
        key = lax.broadcasted_iota(jnp.int32, (2 * keys_img, 1), 0)
        tile_rows = keys_img // MAXT
        live_to = jnp.where(key < keys_img, tiles[0] * tile_rows, keys_img + tiles[1] * tile_rows)
        bias = jnp.where(key < live_to, 0.0, -jnp.inf).astype(F32)
        rows = rows_of(seq)
        both = jnp.concatenate(
            [
                jnp.concatenate(
                    [q_all[rows, h * HD : (h + 1) * HD], g_all[rows, h * HD : (h + 1) * HD]], axis=1
                )
                for h in range(groups)
            ],
            axis=0,
        )
        wide = lax.dot_general(key_val, both, (((1,), (1,)), ((), ())), preferred_element_type=F32)
        return val_key, both, wide[: 2 * keys_img] + bias, wide[2 * keys_img :]

    def finish(seq, state):
        val_key, both, scores, grad_probs = state
        token = lax.broadcasted_iota(jnp.int32, (1, groups * seq_len), 1)
        live = token % seq_len < lengths[seq]
        top = jnp.max(scores, axis=0, keepdims=True)
        expo = jnp.exp2((scores - top) * scale)
        probs = expo * jnp.where(live, 1.0 / jnp.sum(expo, axis=0, keepdims=True), 0.0)
        probs_low = probs.astype(BF16)
        delta = jnp.sum(probs_low.astype(F32) * grad_probs, axis=0, keepdims=True)
        scores_low = (probs * (grad_probs - delta)).astype(BF16)
        low = jnp.concatenate([probs_low, scores_low], axis=0)
        back = jnp.dot(low, both, preferred_element_type=F32)
        result = lax.dot_general(low, val_key, (((0,), (0,)), ((), ())), preferred_element_type=F32)
        rows = rows_of(seq)
        for h in range(groups):
            part = result[h * seq_len : (h + 1) * seq_len]
            out_all[rows, h * HD : (h + 1) * HD] = part[:, :HD].astype(BF16)
            dq_all[rows, h * HD : (h + 1) * HD] = (part[:, HD:] * inv_root).astype(BF16)
        for copy in copies(seq, (2, 3)):
            copy.start()
        val_grad = back[: 2 * keys_img, HD:].astype(BF16)
        key_grad = (back[2 * keys_img :, :HD] * inv_root).astype(BF16)
        for pick in range(2):
            part = slice(pick * keys_img, (pick + 1) * keys_img)
            pair_grad[2 * seq + pick] = jnp.concatenate([key_grad[part], val_grad[part]], axis=1)
            pair_copy(seq, pick).start()

    for seq in range(seq_dev):
        for copy in copies(seq, (0, 1)):
            copy.start()

    @pl.loop(0, seq_dev // unroll)
    def _(turn):
        state = begin(turn * unroll)
        for step in range(unroll):
            seq = turn * unroll + step
            after = begin(seq + 1) if step + 1 < unroll else None
            finish(seq, state)
            state = after

    for seq in range(seq_dev):
        for copy in copies(seq, (2, 3)):
            copy.wait()
        for pick in range(2):
            pair_copy(seq, pick).wait()


def pack_kernel(place, after, features, *rest):
    del after
    *outs, sems = rest
    x_at, z_at, core = place[0], place[1], place[2]
    width = outs[0].shape[1] // SIDE
    copies = []
    for step, out in enumerate(outs):
        for k in range(SIDE):
            low = (lax.rem(x_at + step + 1, SIDE) * SIDE + k) * (2 * width)
            high = (k * SIDE + lax.rem(z_at + step + 1, SIDE)) * (2 * width) + width
            start = pl.multiple_of(jnp.where(core == 0, low, high), width)
            copies.append(
                pltpu.make_async_copy(
                    features.at[:, pl.ds(start, width)],
                    out.at[:, pl.ds(k * width, width)],
                    sems.at[step, k],
                )
            )
    for copy in copies:
        copy.start()
    for copy in copies:
        copy.wait()


def image_kernel(table, slot_grad, grad_low, image_grad):
    slot_total, keys_img, cols = slot_grad.shape
    image_grad[...] = jnp.zeros_like(image_grad)
    for slot in range(slot_total):
        image = table[slot // CAP, slot % CAP]

        @pl.when(image > 0)
        def _():
            image_grad[image - 1] += slot_grad[slot].astype(F32)

    total = image_grad[...].reshape(image_grad.shape[0] * keys_img, cols)
    grad_low[...] = total.T.astype(BF16)


def weight_kernel(place, *refs, half):
    grads, features, sources = refs[:SIDE], refs[SIDE], refs[SIDE + 1 : 3 * SIDE - 1]
    outs = refs[3 * SIDE - 1 : 4 * SIDE - 1]
    rows, total, sems = refs[4 * SIDE - 1 :]
    x_at, z_at, core = place[0], place[1], place[2]
    width = rows.shape[2] // SIDE

    def own_copy(k):
        if half == 0:
            start = (x_at * SIDE + k) * (2 * width)
        else:
            start = (k * SIDE + z_at) * (2 * width) + width
        return pltpu.make_async_copy(
            features.at[:, pl.ds(pl.multiple_of(start, width), width)],
            rows.at[0, :, pl.ds(k * width, width)],
            sems.at[k],
        )

    def far_copy(step, source):
        return pltpu.make_async_copy(source, rows.at[step + 1], sems.at[SIDE + step])

    for k in range(SIDE):
        own_copy(k).start()
    for at, part in ((half, sources[: SIDE - 1]), (1 - half, sources[SIDE - 1 :])):

        @pl.when(core == at)
        def _():
            for step in range(SIDE - 1):
                far_copy(step, part[step]).start()

    for k in range(SIDE):
        own_copy(k).wait()
    for index in range(SIDE):
        if index:
            far_copy(index - 1, sources[index - 1]).wait()
        for k in range(SIDE):
            part = jnp.dot(
                grads[index][...],
                rows[index, :, k * width : (k + 1) * width],
                preferred_element_type=F32,
            )
            if index:
                total[k] += part
            else:
                total[k] = part
    for step in range(SIDE):
        piece = total[lax.rem(place[1 - half] + step, SIDE)]
        outs[step][...] = piece.astype(outs[step].dtype)


def final_kernel(*refs):
    out = refs[-1]
    width = refs[0].shape[1]
    for half in range(2):
        own, one, two, three = refs[4 * half : 4 * half + 4]
        total = own[...] + one[...].astype(F32) + two[...].astype(F32) + three[...].astype(F32)
        for kind in range(2):
            out[half * width : (half + 1) * width, kind, :] = total[kind * HD : (kind + 1) * HD].T


def shift(values, axis, step):
    pairs = []
    for x in range(SIDE):
        for z in range(SIDE):
            to = ((x + step) % SIDE, z) if axis == "x" else (x, (z + step) % SIDE)
            pairs.append((x * SIDE + z, to[0] * SIDE + to[1]))
    return lax.ppermute(values, "txt", pairs)


def feature_shift(values, step):
    pairs = []
    for img in range(lax.axis_size("img")):
        for x in range(SIDE):
            for z in range(SIDE):
                to = ((x + step) % SIDE, z) if img % 2 == 0 else (x, (z + step) % SIDE)
                side = SIDE * SIDE
                pairs.append((img * side + x * SIDE + z, img * side + to[0] * SIDE + to[1]))
    return lax.ppermute(values, ("img", "txt"), pairs)


def swap_cores(values):
    return lax.ppermute(values, "img", [(i, i ^ 1) for i in range(lax.axis_size("img"))])


def shards(features, tile_count, kv_weight, queries, out_grad, image_ids, text_len):
    txt_count = lax.axis_size("txt")
    shard_index = lax.axis_index("txt")
    img_dev, keys_img, feat_width = features.shape
    seq_dev, picks = image_ids.shape
    head_cols = kv_weight.shape[2]
    cols = 2 * head_cols
    request_total = seq_dev * picks
    slot_total = txt_count * CAP
    whole = pl.BlockSpec(memory_space=pltpu.VMEM)
    scalars = pl.BlockSpec(memory_space=pltpu.SMEM)
    in_hbm = pl.BlockSpec(memory_space=pltpu.HBM)

    def params(mib):
        return pltpu.CompilerParams(vmem_limit_bytes=mib * MIB)


    wanted, meta = pl.pallas_call(
        functools.partial(request_kernel, img_dev=img_dev),
        out_shape=[
            jax.ShapeDtypeStruct((txt_count, 128), jnp.int32),
            jax.ShapeDtypeStruct((2 * request_total,), jnp.int32),
        ],
        in_specs=[scalars, scalars],
        out_specs=[whole, scalars],
        scratch_shapes=[pltpu.SMEM((txt_count,), jnp.int32)],
        name="request_table",
    )(image_ids.T, tile_count)
    table = lax.all_to_all(wanted, "txt", 0, 0, tiled=True)
    place = jnp.stack([shard_index // SIDE, shard_index % SIDE, lax.axis_index("img") % 2])

    flat_features = features.reshape(img_dev * keys_img, feat_width)
    own_pairs = jnp.dot(
        flat_features, kv_weight.reshape(feat_width, cols), preferred_element_type=F32
    ).astype(BF16)
    sent_pairs = pl.pallas_call(
        fill_kernel,
        out_shape=jax.ShapeDtypeStruct((slot_total, keys_img, cols), BF16),
        in_specs=[scalars, whole],
        out_specs=in_hbm,
        scratch_shapes=[pltpu.SemaphoreType.DMA((slot_total,))],
        compiler_params=params(8),
        name="fill_slots",
    )(table, own_pairs.reshape(img_dev, keys_img, cols))
    got_pairs = lax.all_to_all(
        sent_pairs.reshape(txt_count, CAP, keys_img, cols), "txt", 0, 0, tiled=True
    ).reshape(slot_total, keys_img, cols)

    block = feat_width // txt_count
    width = block // 2
    held_features = pltpu.with_memory_space_constraint(flat_features, pltpu.HBM)
    messages = pl.pallas_call(
        pack_kernel,
        out_shape=[jax.ShapeDtypeStruct((img_dev * keys_img, SIDE * width), BF16)] * (SIDE - 1),
        in_specs=[scalars, in_hbm, in_hbm],
        out_specs=[whole] * (SIDE - 1),
        scratch_shapes=[pltpu.SemaphoreType.DMA((SIDE - 1, SIDE))],
        compiler_params=params(4),
        cost_estimate=pl.CostEstimate(
            flops=0, bytes_accessed=2 * flat_features.size, transcendentals=0
        ),
        name="pack_features",
    )(place, sent_pairs, held_features)
    got_features = [feature_shift(part, step + 1) for step, part in enumerate(messages)]
    swapped_features = [swap_cores(part) for part in got_features]
    attended, grad_query, slot_grad = pl.pallas_call(
        functools.partial(attend_kernel, img_dev=img_dev),
        out_shape=[
            jax.ShapeDtypeStruct(queries.shape, BF16),
            jax.ShapeDtypeStruct(queries.shape, BF16),
            jax.ShapeDtypeStruct((slot_total, keys_img, cols), BF16),
        ],
        in_specs=[scalars, scalars, scalars, in_hbm, in_hbm, whole],
        out_specs=[in_hbm] * 3,
        scratch_shapes=[pltpu.VMEM(queries.shape, BF16)] * 4
        + [
            pltpu.VMEM((request_total, keys_img, cols), BF16),
            pltpu.SemaphoreType.DMA((4, seq_dev)),
            pltpu.SemaphoreType.DMA((request_total,)),
        ],
        compiler_params=params(24),
        name="attend",
    )(meta, table, text_len, *[pltpu.with_memory_space_constraint(x, pltpu.HBM) for x in (queries, out_grad)], got_pairs)
    back_grad = lax.all_to_all(
        slot_grad.reshape(txt_count, CAP, keys_img, cols), "txt", 0, 0, tiled=True
    ).reshape(slot_total, keys_img, cols)

    grad_low = pl.pallas_call(
        image_kernel,
        out_shape=jax.ShapeDtypeStruct((cols, img_dev * keys_img), BF16),
        in_specs=[scalars, whole],
        out_specs=whole,
        scratch_shapes=[pltpu.VMEM((img_dev, keys_img, cols), F32)],
        compiler_params=params(8),
        name="image_grads",
    )(table, back_grad)
    along = {
        (half, step): shift(grad_low, "xz"[half], step) for step in (2, 1, 3) for half in range(2)
    }
    final = []
    for half in range(2):
        own, *others = pl.pallas_call(
            functools.partial(weight_kernel, half=half),
            out_shape=[
                jax.ShapeDtypeStruct((cols, width), F32 if step == 0 else BF16)
                for step in range(SIDE)
            ],
            in_specs=[scalars] + [whole] * SIDE + [in_hbm] * (2 * SIDE - 1),
            out_specs=[whole] * SIDE,
            scratch_shapes=[
                pltpu.VMEM((SIDE, img_dev * keys_img, SIDE * width), BF16),
                pltpu.VMEM((SIDE, cols, width), F32),
                pltpu.SemaphoreType.DMA((2 * SIDE,)),
            ],
            compiler_params=params(12),
            name="weight_part",
        )(
            place,
            grad_low,
            *[along[half, step] for step in range(1, SIDE)],
            held_features,
            *got_features,
            *swapped_features,
        )
        final += [own] + [shift(part, "zx"[half], step + 1) for step, part in enumerate(others)]
    weight_grad = pl.pallas_call(
        final_kernel,
        out_shape=jax.ShapeDtypeStruct((block, 2, head_cols), F32),
        in_specs=[whole] * 8,
        out_specs=whole,
        compiler_params=params(8),
        name="weight_total",
    )(*final)
    return attended, grad_query, weight_grad


def solution(mesh):
    in_specs = (
        P("txt", None, None),
        P("txt"),
        P(None, None, "img"),
        P("txt", "img"),
        P("txt", "img"),
        P("txt", None),
        P("txt"),
    )
    out_specs = (P("txt", "img"), P("txt", "img"), P("txt", None, "img"))
    return jax.shard_map(shards, mesh=mesh, in_specs=in_specs, out_specs=out_specs, check_vma=False)
```

```python
import functools
import math

import jax
import jax.numpy as jnp
from jax import lax
from jax.experimental import pallas as pl
from jax.experimental.pallas import tpu as pltpu
from jax.sharding import PartitionSpec as P

HD = 128
MAXT = 4
SIDE = 4
CAP = 2
BF16 = jnp.bfloat16
F32 = jnp.float32
MIB = 1024 * 1024


def request_kernel(ids, counts, table, meta, seen, *, img_dev):
    shards, lanes = table.shape
    picks, seq_dev = ids.shape
    for shard in range(shards):
        seen[shard] = 0
    row = lax.broadcasted_iota(jnp.int32, (shards, lanes), 0)
    lane = lax.broadcasted_iota(jnp.int32, (shards, lanes), 1)
    value = jnp.zeros((shards, lanes), jnp.int32)
    for image in range(img_dev):
        value = jnp.where(lane == 8 + image, counts[image], value)
    for request in range(picks * seq_dev):
        image = ids[request % picks, request // picks]
        shard = image // img_dev
        position = seen[shard]
        seen[shard] = position + 1
        value = jnp.where(
            jnp.logical_and(row == shard, lane == position), image % img_dev + 1, value
        )
        meta[request] = shard * CAP + position
        meta[picks * seq_dev + request] = image
    table[...] = value


def fill_kernel(table, pairs, slots, sems):
    copies = []
    for slot in range(slots.shape[0]):
        image = jnp.maximum(table[slot // CAP, slot % CAP] - 1, 0)
        copies.append(pltpu.make_async_copy(pairs.at[image], slots.at[slot], sems.at[slot]))
    for copy in copies:
        copy.start()
    for copy in copies:
        copy.wait()


def attend_kernel(meta, table, lengths, queries, grads, slots, attn, query_grad, slot_grad, *scratch, img_dev):
    q_all, g_all, out_all, dq_all, pair_grad, sems, pair_sems = scratch
    seq_dev = lengths.shape[0]
    seq_len = queries.shape[0] // seq_dev
    groups = queries.shape[1] // HD
    keys_img = slots.shape[1]
    inv_root = 1.0 / math.sqrt(HD)
    scale = inv_root * math.log2(math.e)
    unroll = 6

    def rows_of(seq):
        return pl.ds(pl.multiple_of(seq * seq_len, seq_len), seq_len)

    ends = ((queries, q_all), (grads, g_all), (out_all, attn), (dq_all, query_grad))

    def copies(seq, kinds):
        rows = rows_of(seq)
        return [
            pltpu.make_async_copy(
                ends[kind][0].at[rows], ends[kind][1].at[rows], sems.at[kind, seq]
            )
            for kind in kinds
        ]

    def pair_copy(seq, pick):
        at = 2 * seq + pick
        return pltpu.make_async_copy(
            pair_grad.at[at], slot_grad.at[meta[at]], pair_sems.at[at]
        )

    def begin(seq):
        for copy in copies(seq, (0, 1)):
            copy.wait()
        slot_ids = [meta[2 * seq + pick] for pick in range(2)]
        images = [meta[2 * seq_dev + 2 * seq + pick] for pick in range(2)]
        tiles = [table[image // img_dev, 8 + image % img_dev] for image in images]
        pair = [slots[slot] for slot in slot_ids]
        keys = jnp.concatenate([blk[:, :HD] for blk in pair], axis=0)
        vals = jnp.concatenate([blk[:, HD:] for blk in pair], axis=0)
        none = jnp.zeros_like(keys)
        key_val = jnp.concatenate(
            [jnp.concatenate([keys, none], axis=1), jnp.concatenate([none, vals], axis=1)], axis=0
        )
        val_key = jnp.concatenate(
            [jnp.concatenate([vals, none], axis=1), jnp.concatenate([none, keys], axis=1)], axis=0
        )
        key = lax.broadcasted_iota(jnp.int32, (2 * keys_img, 1), 0)
        tile_rows = keys_img // MAXT
        live_to = jnp.where(key < keys_img, tiles[0] * tile_rows, keys_img + tiles[1] * tile_rows)
        bias = jnp.where(key < live_to, 0.0, -jnp.inf).astype(F32)
        rows = rows_of(seq)
        both = jnp.concatenate(
            [
                jnp.concatenate(
                    [q_all[rows, h * HD : (h + 1) * HD], g_all[rows, h * HD : (h + 1) * HD]], axis=1
                )
                for h in range(groups)
            ],
            axis=0,
        )
        wide = lax.dot_general(key_val, both, (((1,), (1,)), ((), ())), preferred_element_type=F32)
        return val_key, both, wide[: 2 * keys_img] + bias, wide[2 * keys_img :]

    def finish(seq, state):
        val_key, both, scores, grad_probs = state
        token = lax.broadcasted_iota(jnp.int32, (1, groups * seq_len), 1)
        live = token % seq_len < lengths[seq]
        top = jnp.max(scores, axis=0, keepdims=True)
        expo = jnp.exp2((scores - top) * scale)
        probs = expo * jnp.where(live, 1.0 / jnp.sum(expo, axis=0, keepdims=True), 0.0)
        probs_low = probs.astype(BF16)
        delta = jnp.sum(probs_low.astype(F32) * grad_probs, axis=0, keepdims=True)
        scores_low = (probs * (grad_probs - delta)).astype(BF16)
        low = jnp.concatenate([probs_low, scores_low], axis=0)
        back = jnp.dot(low, both, preferred_element_type=F32)
        result = lax.dot_general(low, val_key, (((0,), (0,)), ((), ())), preferred_element_type=F32)
        rows = rows_of(seq)
        for h in range(groups):
            part = result[h * seq_len : (h + 1) * seq_len]
            out_all[rows, h * HD : (h + 1) * HD] = part[:, :HD].astype(BF16)
            dq_all[rows, h * HD : (h + 1) * HD] = (part[:, HD:] * inv_root).astype(BF16)
        for copy in copies(seq, (2, 3)):
            copy.start()
        val_grad = back[: 2 * keys_img, HD:].astype(BF16)
        key_grad = (back[2 * keys_img :, :HD] * inv_root).astype(BF16)
        for pick in range(2):
            part = slice(pick * keys_img, (pick + 1) * keys_img)
            pair_grad[2 * seq + pick] = jnp.concatenate([key_grad[part], val_grad[part]], axis=1)
            pair_copy(seq, pick).start()

    for seq in range(seq_dev):
        for copy in copies(seq, (0, 1)):
            copy.start()

    @pl.loop(0, seq_dev // unroll)
    def _(turn):
        state = begin(turn * unroll)
        for step in range(unroll):
            seq = turn * unroll + step
            after = begin(seq + 1) if step + 1 < unroll else None
            finish(seq, state)
            state = after

    for seq in range(seq_dev):
        for copy in copies(seq, (2, 3)):
            copy.wait()
        for pick in range(2):
            pair_copy(seq, pick).wait()


def pack_kernel(place, after, features, *rest):
    del after
    *outs, sems = rest
    x_at, z_at, core = place[0], place[1], place[2]
    width = outs[0].shape[1] // SIDE
    copies = []
    for step, out in enumerate(outs):
        for k in range(SIDE):
            low = (lax.rem(x_at + step + 1, SIDE) * SIDE + k) * (2 * width)
            high = (k * SIDE + lax.rem(z_at + step + 1, SIDE)) * (2 * width) + width
            start = pl.multiple_of(jnp.where(core == 0, low, high), width)
            count = out.shape[0]
            first = pl.multiple_of(place[3] * count if step == 1 else 0, count)
            copies.append(
                pltpu.make_async_copy(
                    features.at[pl.ds(first, count), pl.ds(start, width)],
                    out.at[:, pl.ds(k * width, width)],
                    sems.at[step, k],
                )
            )
    for copy in copies:
        copy.start()
    for copy in copies:
        copy.wait()


def image_kernel(table, slot_grad, grad_low, image_grad):
    slot_total, keys_img, cols = slot_grad.shape
    image_grad[...] = jnp.zeros_like(image_grad)
    for slot in range(slot_total):
        image = table[slot // CAP, slot % CAP]

        @pl.when(image > 0)
        def _():
            image_grad[image - 1] += slot_grad[slot].astype(F32)

    total = image_grad[...].reshape(image_grad.shape[0] * keys_img, cols)
    grad_low[...] = total.T.astype(BF16)


def near_kernel(place, grad_low, features, *rest):
    sources, (grad_again, rows, sems) = rest[:-3], rest[-3:]
    x_at, z_at, core = place[0], place[1], place[2]
    width = rows.shape[3] // SIDE

    def own_copy(half, k):
        if half == 0:
            start = (x_at * SIDE + k) * (2 * width)
        else:
            start = (k * SIDE + z_at) * (2 * width) + width
        return pltpu.make_async_copy(
            features.at[:, pl.ds(pl.multiple_of(start, width), width)],
            rows.at[half, 0, :, pl.ds(k * width, width)],
            sems.at[half, k],
        )

    def far_copy(half, index, source):
        to = rows.at[half, (1, 2, 2, 3)[index]]
        if index in (1, 2):
            count = source.shape[0]
            first = place[3] if index == 1 else 1 - place[3]
            to = to.at[pl.ds(pl.multiple_of(first * count, count), count)]
        return pltpu.make_async_copy(source, to, sems.at[half, SIDE + index])

    far = len(sources) // 2
    for half in range(2):
        for k in range(SIDE):
            own_copy(half, k).start()
        for at, part in ((half, sources[:far]), (1 - half, sources[far:])):

            @pl.when(core == at)
            def _():
                for step in range(far):
                    far_copy(half, step, part[step]).start()

    grad_again[...] = grad_low[...]
    for half in range(2):
        for k in range(SIDE):
            own_copy(half, k).wait()
        for step in range(far):
            far_copy(half, step, sources[step]).wait()


def weight_kernel(place, *refs, half):
    grads, rows, outs = refs[:SIDE], refs[SIDE], refs[SIDE + 1 :]
    width = rows.shape[3] // SIDE
    for step in range(SIDE):
        start = pl.multiple_of(lax.rem(place[1 - half] + step, SIDE) * width, width)
        total = None
        for index in range(SIDE):
            part = jnp.dot(
                grads[index][...],
                rows[half, index, :, pl.ds(start, width)],
                preferred_element_type=F32,
            )
            total = part if index == 0 else total + part
        outs[step][...] = total.astype(outs[step].dtype)


def final_kernel(*refs):
    out = refs[-1]
    width = refs[0].shape[1]
    for half in range(2):
        own, one, two, three = refs[4 * half : 4 * half + 4]
        total = own[...] + one[...].astype(F32) + two[...].astype(F32) + three[...].astype(F32)
        for kind in range(2):
            out[half * width : (half + 1) * width, kind, :] = total[kind * HD : (kind + 1) * HD].T


def shift(values, axis, step):
    pairs = []
    for x in range(SIDE):
        for z in range(SIDE):
            to = ((x + step) % SIDE, z) if axis == "x" else (x, (z + step) % SIDE)
            pairs.append((x * SIDE + z, to[0] * SIDE + to[1]))
    return lax.ppermute(values, "txt", pairs)


def feature_shift(values, step):
    pairs = []
    for img in range(lax.axis_size("img")):
        for x in range(SIDE):
            for z in range(SIDE):
                to = ((x + step) % SIDE, z) if img % 2 == 0 else (x, (z + step) % SIDE)
                side = SIDE * SIDE
                pairs.append((img * side + x * SIDE + z, img * side + to[0] * SIDE + to[1]))
    return lax.ppermute(values, ("img", "txt"), pairs)


def swap_img(values, bit):
    return lax.ppermute(values, "img", [(i, i ^ bit) for i in range(lax.axis_size("img"))])


def shards(features, tile_count, kv_weight, queries, out_grad, image_ids, text_len):
    txt_count = lax.axis_size("txt")
    shard_index = lax.axis_index("txt")
    img_dev, keys_img, feat_width = features.shape
    seq_dev, picks = image_ids.shape
    head_cols = kv_weight.shape[2]
    cols = 2 * head_cols
    request_total = seq_dev * picks
    slot_total = txt_count * CAP
    whole = pl.BlockSpec(memory_space=pltpu.VMEM)
    scalars = pl.BlockSpec(memory_space=pltpu.SMEM)
    in_hbm = pl.BlockSpec(memory_space=pltpu.HBM)

    def params(mib):
        return pltpu.CompilerParams(vmem_limit_bytes=mib * MIB)


    wanted, meta = pl.pallas_call(
        functools.partial(request_kernel, img_dev=img_dev),
        out_shape=[
            jax.ShapeDtypeStruct((txt_count, 128), jnp.int32),
            jax.ShapeDtypeStruct((2 * request_total,), jnp.int32),
        ],
        in_specs=[scalars, scalars],
        out_specs=[whole, scalars],
        scratch_shapes=[pltpu.SMEM((txt_count,), jnp.int32)],
        name="request_table",
    )(image_ids.T, tile_count)
    table = lax.all_to_all(wanted, "txt", 0, 0, tiled=True)
    place = jnp.stack([shard_index // SIDE, shard_index % SIDE, lax.axis_index("img") % 2, lax.axis_index("img") // 2 % 2])

    flat_features = features.reshape(img_dev * keys_img, feat_width)
    own_pairs = jnp.dot(
        flat_features, kv_weight.reshape(feat_width, cols), preferred_element_type=F32
    ).astype(BF16)
    sent_pairs = pl.pallas_call(
        fill_kernel,
        out_shape=jax.ShapeDtypeStruct((slot_total, keys_img, cols), BF16),
        in_specs=[scalars, whole],
        out_specs=in_hbm,
        scratch_shapes=[pltpu.SemaphoreType.DMA((slot_total,))],
        compiler_params=params(8),
        name="fill_slots",
    )(table, own_pairs.reshape(img_dev, keys_img, cols))
    got_pairs = lax.all_to_all(
        sent_pairs.reshape(txt_count, CAP, keys_img, cols), "txt", 0, 0, tiled=True
    ).reshape(slot_total, keys_img, cols)

    block = feat_width // txt_count
    width = block // 2
    held_rows = img_dev * keys_img
    held_features = pltpu.with_memory_space_constraint(flat_features, pltpu.HBM)
    messages = pl.pallas_call(
        pack_kernel,
        out_shape=[
            jax.ShapeDtypeStruct((count, SIDE * width), BF16)
            for count in (held_rows, held_rows // 2, held_rows)
        ],
        in_specs=[scalars, in_hbm, in_hbm],
        out_specs=[whole] * (SIDE - 1),
        scratch_shapes=[pltpu.SemaphoreType.DMA((SIDE - 1, SIDE))],
        compiler_params=params(4),
        cost_estimate=pl.CostEstimate(
            flops=0, bytes_accessed=2 * flat_features.size, transcendentals=0
        ),
        name="pack_features",
    )(place, sent_pairs, held_features)
    got_features = [feature_shift(part, step + 1) for step, part in enumerate(messages)]
    got_features.insert(2, swap_img(got_features[1], 2))
    swapped_features = [swap_img(part, 1) for part in got_features]
    attended, grad_query, slot_grad = pl.pallas_call(
        functools.partial(attend_kernel, img_dev=img_dev),
        out_shape=[
            jax.ShapeDtypeStruct(queries.shape, BF16),
            jax.ShapeDtypeStruct(queries.shape, BF16),
            jax.ShapeDtypeStruct((slot_total, keys_img, cols), BF16),
        ],
        in_specs=[scalars, scalars, scalars, in_hbm, in_hbm, whole],
        out_specs=[in_hbm] * 3,
        scratch_shapes=[pltpu.VMEM(queries.shape, BF16)] * 4
        + [
            pltpu.VMEM((request_total, keys_img, cols), BF16),
            pltpu.SemaphoreType.DMA((4, seq_dev)),
            pltpu.SemaphoreType.DMA((request_total,)),
        ],
        compiler_params=params(24),
        name="attend",
    )(meta, table, text_len, *[pltpu.with_memory_space_constraint(x, pltpu.HBM) for x in (queries, out_grad)], got_pairs)
    back_grad = lax.all_to_all(
        slot_grad.reshape(txt_count, CAP, keys_img, cols), "txt", 0, 0, tiled=True
    ).reshape(slot_total, keys_img, cols)

    grad_low = pl.pallas_call(
        image_kernel,
        out_shape=jax.ShapeDtypeStruct((cols, img_dev * keys_img), BF16),
        in_specs=[scalars, whole],
        out_specs=whole,
        scratch_shapes=[pltpu.VMEM((img_dev, keys_img, cols), F32)],
        compiler_params=params(8),
        name="image_grads",
    )(table, back_grad)
    grad_again, near = pl.pallas_call(
        near_kernel,
        out_shape=[
            jax.ShapeDtypeStruct(grad_low.shape, BF16),
            jax.ShapeDtypeStruct((2, SIDE, img_dev * keys_img, SIDE * width), BF16),
        ],
        in_specs=[scalars, whole] + [in_hbm] * (2 * SIDE + 1),
        out_specs=[whole] * 2,
        scratch_shapes=[pltpu.SemaphoreType.DMA((2, 2 * SIDE))],
        compiler_params=params(4),
        cost_estimate=pl.CostEstimate(
            flops=0, bytes_accessed=2 * flat_features.size, transcendentals=0
        ),
        name="near_features",
    )(place, grad_low, held_features, *got_features, *swapped_features)
    along = {
        (half, step): shift(grad_again if (half, step) == (1, 3) else grad_low, "xz"[half], step)
        for step in (2, 1, 3)
        for half in range(2)
    }
    final = []
    for half in range(2):
        own, *others = pl.pallas_call(
            functools.partial(weight_kernel, half=half),
            out_shape=[
                jax.ShapeDtypeStruct((cols, width), F32 if step == 0 else BF16)
                for step in range(SIDE)
            ],
            in_specs=[scalars] + [whole] * (SIDE + 1),
            out_specs=[whole] * SIDE,
            compiler_params=params(8),
            name="weight_part",
        )(place, grad_low, *[along[half, step] for step in range(1, SIDE)], near)
        final += [own] + [shift(part, "zx"[half], step + 1) for step, part in enumerate(others)]
    weight_grad = pl.pallas_call(
        final_kernel,
        out_shape=jax.ShapeDtypeStruct((block, 2, head_cols), F32),
        in_specs=[whole] * 8,
        out_specs=whole,
        compiler_params=params(8),
        name="weight_total",
    )(*final)
    return attended, grad_query, weight_grad


def solution(mesh):
    in_specs = (
        P("txt", None, None),
        P("txt"),
        P(None, None, "img"),
        P("txt", "img"),
        P("txt", "img"),
        P("txt", None),
        P("txt"),
    )
    out_specs = (P("txt", "img"), P("txt", "img"), P("txt", None, "img"))
    return jax.shard_map(shards, mesh=mesh, in_specs=in_specs, out_specs=out_specs, check_vma=False)
```

```python
import functools
import math

import jax
import jax.numpy as jnp
from jax import lax
from jax.experimental import pallas as pl
from jax.experimental.pallas import tpu as pltpu
from jax.sharding import PartitionSpec as P

HD = 128
MAXT = 4
SIDE = 4
CAP = 2
BF16 = jnp.bfloat16
F32 = jnp.float32
MIB = 1024 * 1024


def request_kernel(ids, counts, table, meta, seen, *, img_dev):
    shards, lanes = table.shape
    picks, seq_dev = ids.shape
    for shard in range(shards):
        seen[shard] = 0
    row = lax.broadcasted_iota(jnp.int32, (shards, lanes), 0)
    lane = lax.broadcasted_iota(jnp.int32, (shards, lanes), 1)
    value = jnp.zeros((shards, lanes), jnp.int32)
    for image in range(img_dev):
        value = jnp.where(lane == 8 + image, counts[image], value)
    for request in range(picks * seq_dev):
        image = ids[request % picks, request // picks]
        shard = image // img_dev
        position = seen[shard]
        seen[shard] = position + 1
        value = jnp.where(
            jnp.logical_and(row == shard, lane == position), image % img_dev + 1, value
        )
        meta[request] = shard * CAP + position
        meta[picks * seq_dev + request] = image
    table[...] = value


def fill_kernel(table, pairs, slots):
    for slot in range(slots.shape[0]):
        image = jnp.maximum(table[slot // CAP, slot % CAP] - 1, 0)
        slots[slot] = pairs[image]


def attend_kernel(meta, table, lengths, queries, grads, slots, attn, query_grad, slot_grad, *scratch, img_dev):
    q_all, g_all, out_all, dq_all, sems = scratch
    seq_dev = lengths.shape[0]
    seq_len = queries.shape[0] // seq_dev
    groups = queries.shape[1] // HD
    keys_img = slots.shape[1]
    inv_root = 1.0 / math.sqrt(HD)
    scale = inv_root * math.log2(math.e)
    unroll = 6

    def rows_of(seq):
        return pl.ds(pl.multiple_of(seq * seq_len, seq_len), seq_len)

    ends = ((queries, q_all), (grads, g_all), (out_all, attn), (dq_all, query_grad))

    def copies(seq, kinds):
        rows = rows_of(seq)
        return [
            pltpu.make_async_copy(
                ends[kind][0].at[rows], ends[kind][1].at[rows], sems.at[kind, seq]
            )
            for kind in kinds
        ]

    def begin(seq):
        for copy in copies(seq, (0, 1)):
            copy.wait()
        slot_ids = [meta[2 * seq + pick] for pick in range(2)]
        images = [meta[2 * seq_dev + 2 * seq + pick] for pick in range(2)]
        tiles = [table[image // img_dev, 8 + image % img_dev] for image in images]
        pair = [slots[slot] for slot in slot_ids]
        keys = jnp.concatenate([blk[:, :HD] for blk in pair], axis=0)
        vals = jnp.concatenate([blk[:, HD:] for blk in pair], axis=0)
        none = jnp.zeros_like(keys)
        key_val = jnp.concatenate(
            [jnp.concatenate([keys, none], axis=1), jnp.concatenate([none, vals], axis=1)], axis=0
        )
        val_key = jnp.concatenate(
            [jnp.concatenate([vals, none], axis=1), jnp.concatenate([none, keys], axis=1)], axis=0
        )
        key = lax.broadcasted_iota(jnp.int32, (2 * keys_img, 1), 0)
        tile_rows = keys_img // MAXT
        live_to = jnp.where(key < keys_img, tiles[0] * tile_rows, keys_img + tiles[1] * tile_rows)
        bias = jnp.where(key < live_to, 0.0, -jnp.inf).astype(F32)
        rows = rows_of(seq)
        both = jnp.concatenate(
            [
                jnp.concatenate(
                    [q_all[rows, h * HD : (h + 1) * HD], g_all[rows, h * HD : (h + 1) * HD]], axis=1
                )
                for h in range(groups)
            ],
            axis=0,
        )
        wide = lax.dot_general(key_val, both, (((1,), (1,)), ((), ())), preferred_element_type=F32)
        return slot_ids, val_key, both, wide[: 2 * keys_img] + bias, wide[2 * keys_img :]

    def finish(seq, state):
        slot_ids, val_key, both, scores, grad_probs = state
        token = lax.broadcasted_iota(jnp.int32, (1, groups * seq_len), 1)
        live = token % seq_len < lengths[seq]
        top = jnp.max(scores, axis=0, keepdims=True)
        expo = jnp.exp2((scores - top) * scale)
        probs = expo * jnp.where(live, 1.0 / jnp.sum(expo, axis=0, keepdims=True), 0.0)
        probs_low = probs.astype(BF16)
        delta = jnp.sum(probs_low.astype(F32) * grad_probs, axis=0, keepdims=True)
        scores_low = (probs * (grad_probs - delta)).astype(BF16)
        low = jnp.concatenate([probs_low, scores_low], axis=0)
        back = jnp.dot(low, both, preferred_element_type=F32)
        result = lax.dot_general(low, val_key, (((0,), (0,)), ((), ())), preferred_element_type=F32)
        rows = rows_of(seq)
        for h in range(groups):
            part = result[h * seq_len : (h + 1) * seq_len]
            out_all[rows, h * HD : (h + 1) * HD] = part[:, :HD].astype(BF16)
            dq_all[rows, h * HD : (h + 1) * HD] = (part[:, HD:] * inv_root).astype(BF16)
        for copy in copies(seq, (2, 3)):
            copy.start()
        val_grad = back[: 2 * keys_img, HD:].astype(BF16)
        key_grad = (back[2 * keys_img :, :HD] * inv_root).astype(BF16)
        for pick in range(2):
            part = slice(pick * keys_img, (pick + 1) * keys_img)
            slot_grad[slot_ids[pick]] = jnp.concatenate([key_grad[part], val_grad[part]], axis=1)

    for seq in range(seq_dev):
        for copy in copies(seq, (0, 1)):
            copy.start()

    @pl.loop(0, seq_dev // unroll)
    def _(turn):
        state = begin(turn * unroll)
        for step in range(unroll):
            seq = turn * unroll + step
            after = begin(seq + 1) if step + 1 < unroll else None
            finish(seq, state)
            state = after

    for seq in range(seq_dev):
        for copy in copies(seq, (2, 3)):
            copy.wait()


def pack_kernel(place, after, features, *rest):
    del after
    *outs, sems = rest
    x_at, z_at, core = place[0], place[1], place[2]
    width = outs[0].shape[1] // SIDE
    copies = []
    for step, out in enumerate(outs):
        for k in range(SIDE):
            low = (lax.rem(x_at + step + 1, SIDE) * SIDE + k) * (2 * width)
            high = (k * SIDE + lax.rem(z_at + step + 1, SIDE)) * (2 * width) + width
            start = pl.multiple_of(jnp.where(core == 0, low, high), width)
            count = out.shape[0]
            first = pl.multiple_of(place[3] * count if step == 1 else 0, count)
            copies.append(
                pltpu.make_async_copy(
                    features.at[pl.ds(first, count), pl.ds(start, width)],
                    out.at[:, pl.ds(k * width, width)],
                    sems.at[step, k],
                )
            )
    for copy in copies:
        copy.start()
    for copy in copies:
        copy.wait()


def image_kernel(table, slot_grad, grad_low, image_grad):
    slot_total, keys_img, cols = slot_grad.shape
    image_grad[...] = jnp.zeros_like(image_grad)
    for slot in range(slot_total):
        image = table[slot // CAP, slot % CAP]

        @pl.when(image > 0)
        def _():
            image_grad[image - 1] += slot_grad[slot].astype(F32)

    total = image_grad[...].reshape(image_grad.shape[0] * keys_img, cols)
    grad_low[...] = total.T.astype(BF16)


def near_kernel(place, grad_low, features, *rest):
    sources, (grad_again, rows, sems) = rest[:-3], rest[-3:]
    x_at, z_at, core = place[0], place[1], place[2]
    width = rows.shape[3] // SIDE

    def own_copy(half, k):
        if half == 0:
            start = (x_at * SIDE + k) * (2 * width)
        else:
            start = (k * SIDE + z_at) * (2 * width) + width
        return pltpu.make_async_copy(
            features.at[:, pl.ds(pl.multiple_of(start, width), width)],
            rows.at[half, 0, :, pl.ds(k * width, width)],
            sems.at[half, k],
        )

    def far_copy(half, index, source):
        to = rows.at[half, (1, 2, 2, 3)[index]]
        if index in (1, 2):
            count = source.shape[0]
            first = place[3] if index == 1 else 1 - place[3]
            to = to.at[pl.ds(pl.multiple_of(first * count, count), count)]
        return pltpu.make_async_copy(source, to, sems.at[half, SIDE + index])

    far = len(sources) // 2
    for half in range(2):
        for k in range(SIDE):
            own_copy(half, k).start()
        for at, part in ((half, sources[:far]), (1 - half, sources[far:])):

            @pl.when(core == at)
            def _():
                for step in range(far):
                    far_copy(half, step, part[step]).start()

    grad_again[...] = grad_low[...]
    for half in range(2):
        for k in range(SIDE):
            own_copy(half, k).wait()
        for step in range(far):
            far_copy(half, step, sources[step]).wait()


def weight_kernel(place, *refs, half):
    grads, rows, outs = refs[:SIDE], refs[SIDE], refs[SIDE + 1 :]
    width = rows.shape[3] // SIDE
    for step in range(SIDE):
        start = pl.multiple_of(lax.rem(place[1 - half] + step, SIDE) * width, width)
        total = None
        for index in range(SIDE):
            part = jnp.dot(
                grads[index][...],
                rows[half, index, :, pl.ds(start, width)],
                preferred_element_type=F32,
            )
            total = part if index == 0 else total + part
        outs[step][...] = total.astype(outs[step].dtype)


def final_kernel(*refs):
    out = refs[-1]
    width = refs[0].shape[1]
    for half in range(2):
        own, one, two, three = refs[4 * half : 4 * half + 4]
        total = own[...] + one[...].astype(F32) + two[...].astype(F32) + three[...].astype(F32)
        for kind in range(2):
            out[half * width : (half + 1) * width, kind, :] = total[kind * HD : (kind + 1) * HD].T


def shift(values, axis, step):
    pairs = []
    for x in range(SIDE):
        for z in range(SIDE):
            to = ((x + step) % SIDE, z) if axis == "x" else (x, (z + step) % SIDE)
            pairs.append((x * SIDE + z, to[0] * SIDE + to[1]))
    return lax.ppermute(values, "txt", pairs)


def feature_shift(values, step):
    pairs = []
    for img in range(lax.axis_size("img")):
        for x in range(SIDE):
            for z in range(SIDE):
                to = ((x + step) % SIDE, z) if img % 2 == 0 else (x, (z + step) % SIDE)
                side = SIDE * SIDE
                pairs.append((img * side + x * SIDE + z, img * side + to[0] * SIDE + to[1]))
    return lax.ppermute(values, ("img", "txt"), pairs)


def swap_img(values, bit):
    return lax.ppermute(values, "img", [(i, i ^ bit) for i in range(lax.axis_size("img"))])


def shards(features, tile_count, kv_weight, queries, out_grad, image_ids, text_len):
    txt_count = lax.axis_size("txt")
    shard_index = lax.axis_index("txt")
    img_dev, keys_img, feat_width = features.shape
    seq_dev, picks = image_ids.shape
    head_cols = kv_weight.shape[2]
    cols = 2 * head_cols
    request_total = seq_dev * picks
    slot_total = txt_count * CAP
    whole = pl.BlockSpec(memory_space=pltpu.VMEM)
    scalars = pl.BlockSpec(memory_space=pltpu.SMEM)
    in_hbm = pl.BlockSpec(memory_space=pltpu.HBM)

    def params(mib):
        return pltpu.CompilerParams(vmem_limit_bytes=mib * MIB)


    wanted, meta = pl.pallas_call(
        functools.partial(request_kernel, img_dev=img_dev),
        out_shape=[
            jax.ShapeDtypeStruct((txt_count, 128), jnp.int32),
            jax.ShapeDtypeStruct((2 * request_total,), jnp.int32),
        ],
        in_specs=[scalars, scalars],
        out_specs=[whole, scalars],
        scratch_shapes=[pltpu.SMEM((txt_count,), jnp.int32)],
        name="request_table",
    )(image_ids.T, tile_count)
    table = lax.all_to_all(wanted, "txt", 0, 0, tiled=True)
    place = jnp.stack([shard_index // SIDE, shard_index % SIDE, lax.axis_index("img") % 2, lax.axis_index("img") // 2 % 2])

    flat_features = features.reshape(img_dev * keys_img, feat_width)
    own_pairs = jnp.dot(
        flat_features, kv_weight.reshape(feat_width, cols), preferred_element_type=F32
    ).astype(BF16)
    sent_pairs = pl.pallas_call(
        fill_kernel,
        out_shape=jax.ShapeDtypeStruct((slot_total, keys_img, cols), BF16),
        in_specs=[scalars, whole],
        out_specs=whole,
        compiler_params=params(8),
        name="fill_slots",
    )(table, own_pairs.reshape(img_dev, keys_img, cols))
    got_pairs = lax.all_to_all(
        sent_pairs.reshape(txt_count, CAP, keys_img, cols), "txt", 0, 0, tiled=True
    ).reshape(slot_total, keys_img, cols)

    block = feat_width // txt_count
    width = block // 2
    held_rows = img_dev * keys_img
    held_features = pltpu.with_memory_space_constraint(flat_features, pltpu.HBM)
    messages = pl.pallas_call(
        pack_kernel,
        out_shape=[
            jax.ShapeDtypeStruct((count, SIDE * width), BF16)
            for count in (held_rows, held_rows // 2, held_rows)
        ],
        in_specs=[scalars, in_hbm, in_hbm],
        out_specs=[whole] * (SIDE - 1),
        scratch_shapes=[pltpu.SemaphoreType.DMA((SIDE - 1, SIDE))],
        compiler_params=params(4),
        cost_estimate=pl.CostEstimate(
            flops=0, bytes_accessed=2 * flat_features.size, transcendentals=0
        ),
        name="pack_features",
    )(place, sent_pairs, held_features)
    got_features = [feature_shift(part, step + 1) for step, part in enumerate(messages)]
    got_features.insert(2, swap_img(got_features[1], 2))
    swapped_features = [swap_img(part, 1) for part in got_features]
    attended, grad_query, slot_grad = pl.pallas_call(
        functools.partial(attend_kernel, img_dev=img_dev),
        out_shape=[
            jax.ShapeDtypeStruct(queries.shape, BF16),
            jax.ShapeDtypeStruct(queries.shape, BF16),
            jax.ShapeDtypeStruct((slot_total, keys_img, cols), BF16),
        ],
        in_specs=[scalars, scalars, scalars, in_hbm, in_hbm, whole],
        out_specs=[in_hbm, in_hbm, whole],
        scratch_shapes=[pltpu.VMEM(queries.shape, BF16)] * 4
        + [pltpu.SemaphoreType.DMA((4, seq_dev))],
        compiler_params=params(24),
        name="attend",
    )(meta, table, text_len, *[pltpu.with_memory_space_constraint(x, pltpu.HBM) for x in (queries, out_grad)], got_pairs)
    back_grad = lax.all_to_all(
        slot_grad.reshape(txt_count, CAP, keys_img, cols), "txt", 0, 0, tiled=True
    ).reshape(slot_total, keys_img, cols)

    grad_low = pl.pallas_call(
        image_kernel,
        out_shape=jax.ShapeDtypeStruct((cols, img_dev * keys_img), BF16),
        in_specs=[scalars, whole],
        out_specs=whole,
        scratch_shapes=[pltpu.VMEM((img_dev, keys_img, cols), F32)],
        compiler_params=params(8),
        name="image_grads",
    )(table, back_grad)
    grad_again, near = pl.pallas_call(
        near_kernel,
        out_shape=[
            jax.ShapeDtypeStruct(grad_low.shape, BF16),
            jax.ShapeDtypeStruct((2, SIDE, img_dev * keys_img, SIDE * width), BF16),
        ],
        in_specs=[scalars, whole] + [in_hbm] * (2 * SIDE + 1),
        out_specs=[whole] * 2,
        scratch_shapes=[pltpu.SemaphoreType.DMA((2, 2 * SIDE))],
        compiler_params=params(4),
        cost_estimate=pl.CostEstimate(
            flops=0, bytes_accessed=2 * flat_features.size, transcendentals=0
        ),
        name="near_features",
    )(place, grad_low, held_features, *got_features, *swapped_features)
    along = {
        (half, step): shift(grad_again if (half, step) == (1, 3) else grad_low, "xz"[half], step)
        for step in (2, 1, 3)
        for half in range(2)
    }
    final = []
    for half in range(2):
        own, *others = pl.pallas_call(
            functools.partial(weight_kernel, half=half),
            out_shape=[
                jax.ShapeDtypeStruct((cols, width), F32 if step == 0 else BF16)
                for step in range(SIDE)
            ],
            in_specs=[scalars] + [whole] * (SIDE + 1),
            out_specs=[whole] * SIDE,
            compiler_params=params(8),
            name="weight_part",
        )(place, grad_low, *[along[half, step] for step in range(1, SIDE)], near)
        final += [own] + [shift(part, "zx"[half], step + 1) for step, part in enumerate(others)]
    weight_grad = pl.pallas_call(
        final_kernel,
        out_shape=jax.ShapeDtypeStruct((block, 2, head_cols), F32),
        in_specs=[whole] * 8,
        out_specs=whole,
        compiler_params=params(8),
        name="weight_total",
    )(*final)
    return attended, grad_query, weight_grad


def solution(mesh):
    in_specs = (
        P("txt", None, None),
        P("txt"),
        P(None, None, "img"),
        P("txt", "img"),
        P("txt", "img"),
        P("txt", None),
        P("txt"),
    )
    out_specs = (P("txt", "img"), P("txt", "img"), P("txt", None, "img"))
    return jax.shard_map(shards, mesh=mesh, in_specs=in_specs, out_specs=out_specs, check_vma=False)
```

```python
import functools
import math

import jax
import jax.numpy as jnp
from jax import lax
from jax.experimental import pallas as pl
from jax.experimental.pallas import tpu as pltpu
from jax.sharding import PartitionSpec as P

HD = 128
MAXT = 4
SIDE = 4
CAP = 2
BF16 = jnp.bfloat16
F32 = jnp.float32
MIB = 1024 * 1024


def request_kernel(ids, counts, table, meta, seen, *, img_dev):
    shards, lanes = table.shape
    picks, seq_dev = ids.shape
    for shard in range(shards):
        seen[shard] = 0
    row = lax.broadcasted_iota(jnp.int32, (shards, lanes), 0)
    lane = lax.broadcasted_iota(jnp.int32, (shards, lanes), 1)
    value = jnp.zeros((shards, lanes), jnp.int32)
    for image in range(img_dev):
        value = jnp.where(lane == 8 + image, counts[image], value)
    for request in range(picks * seq_dev):
        image = ids[request % picks, request // picks]
        shard = image // img_dev
        position = seen[shard]
        seen[shard] = position + 1
        value = jnp.where(
            jnp.logical_and(row == shard, lane == position), image % img_dev + 1, value
        )
        meta[request] = shard * CAP + position
        meta[picks * seq_dev + request] = image
    table[...] = value


def fill_kernel(table, pairs, slots):
    for slot in range(slots.shape[0]):
        image = jnp.maximum(table[slot // CAP, slot % CAP] - 1, 0)
        slots[slot] = pairs[image]


def attend_kernel(meta, table, lengths, queries, grads, slots, attn, query_grad, slot_grad, *scratch, img_dev):
    q_all, g_all, out_all, dq_all, sems = scratch
    seq_dev = lengths.shape[0]
    seq_len = queries.shape[0] // seq_dev
    groups = queries.shape[1] // HD
    keys_img = slots.shape[1]
    inv_root = 1.0 / math.sqrt(HD)
    scale = inv_root * math.log2(math.e)
    unroll = 6

    def rows_of(seq):
        return pl.ds(pl.multiple_of(seq * seq_len, seq_len), seq_len)

    ends = ((queries, q_all), (grads, g_all), (out_all, attn), (dq_all, query_grad))

    def copies(seq, kinds):
        rows = rows_of(seq)
        return [
            pltpu.make_async_copy(
                ends[kind][0].at[rows], ends[kind][1].at[rows], sems.at[kind, seq]
            )
            for kind in kinds
        ]

    def begin(seq):
        for copy in copies(seq, (0, 1)):
            copy.wait()
        slot_ids = [meta[2 * seq + pick] for pick in range(2)]
        images = [meta[2 * seq_dev + 2 * seq + pick] for pick in range(2)]
        tiles = [table[image // img_dev, 8 + image % img_dev] for image in images]
        pair = [slots[slot] for slot in slot_ids]
        keys = jnp.concatenate([blk[:, :HD] for blk in pair], axis=0)
        vals = jnp.concatenate([blk[:, HD:] for blk in pair], axis=0)
        none = jnp.zeros_like(keys)
        key_val = jnp.concatenate(
            [jnp.concatenate([keys, none], axis=1), jnp.concatenate([none, vals], axis=1)], axis=0
        )
        val_key = jnp.concatenate(
            [jnp.concatenate([vals, none], axis=1), jnp.concatenate([none, keys], axis=1)], axis=0
        )
        key = lax.broadcasted_iota(jnp.int32, (2 * keys_img, 1), 0)
        tile_rows = keys_img // MAXT
        live_to = jnp.where(key < keys_img, tiles[0] * tile_rows, keys_img + tiles[1] * tile_rows)
        bias = jnp.where(key < live_to, 0.0, -jnp.inf).astype(F32)
        rows = rows_of(seq)
        both = jnp.concatenate(
            [
                jnp.concatenate(
                    [q_all[rows, h * HD : (h + 1) * HD], g_all[rows, h * HD : (h + 1) * HD]], axis=1
                )
                for h in range(groups)
            ],
            axis=0,
        )
        wide = lax.dot_general(key_val, both, (((1,), (1,)), ((), ())), preferred_element_type=F32)
        return slot_ids, val_key, both, wide[: 2 * keys_img] + bias, wide[2 * keys_img :]

    def finish(seq, state):
        slot_ids, val_key, both, scores, grad_probs = state
        token = lax.broadcasted_iota(jnp.int32, (1, groups * seq_len), 1)
        live = token % seq_len < lengths[seq]
        top = jnp.max(scores, axis=0, keepdims=True)
        expo = jnp.exp2((scores - top) * scale)
        probs = expo * jnp.where(live, 1.0 / jnp.sum(expo, axis=0, keepdims=True), 0.0)
        probs_low = probs.astype(BF16)
        delta = jnp.sum(probs_low.astype(F32) * grad_probs, axis=0, keepdims=True)
        scores_low = (probs * (grad_probs - delta)).astype(BF16)
        low = jnp.concatenate([probs_low, scores_low], axis=0)
        back = jnp.dot(low, both, preferred_element_type=F32)
        result = lax.dot_general(low, val_key, (((0,), (0,)), ((), ())), preferred_element_type=F32)
        rows = rows_of(seq)
        for h in range(groups):
            part = result[h * seq_len : (h + 1) * seq_len]
            out_all[rows, h * HD : (h + 1) * HD] = part[:, :HD].astype(BF16)
            dq_all[rows, h * HD : (h + 1) * HD] = (part[:, HD:] * inv_root).astype(BF16)
        for copy in copies(seq, (2, 3)):
            copy.start()
        val_grad = back[: 2 * keys_img, HD:].astype(BF16)
        key_grad = (back[2 * keys_img :, :HD] * inv_root).astype(BF16)
        for pick in range(2):
            part = slice(pick * keys_img, (pick + 1) * keys_img)
            slot_grad[slot_ids[pick]] = jnp.concatenate([key_grad[part], val_grad[part]], axis=1)

    for seq in range(seq_dev):
        for copy in copies(seq, (0, 1)):
            copy.start()

    @pl.loop(0, seq_dev // unroll)
    def _(turn):
        state = begin(turn * unroll)
        for step in range(unroll):
            seq = turn * unroll + step
            after = begin(seq + 1) if step + 1 < unroll else None
            finish(seq, state)
            state = after

    for seq in range(seq_dev):
        for copy in copies(seq, (2, 3)):
            copy.wait()


def pack_kernel(place, after, features, *rest):
    del after
    *outs, sems = rest
    x_at, z_at, core = place[0], place[1], place[2]
    width = outs[0].shape[1] // SIDE
    copies = []
    for step, out in enumerate(outs):
        for k in range(SIDE):
            low = (lax.rem(x_at + step + 1, SIDE) * SIDE + k) * (2 * width)
            high = (k * SIDE + lax.rem(z_at + step + 1, SIDE)) * (2 * width) + width
            start = pl.multiple_of(jnp.where(core == 0, low, high), width)
            count = out.shape[0]
            first = pl.multiple_of(place[3] * count if step == 1 else 0, count)
            copies.append(
                pltpu.make_async_copy(
                    features.at[pl.ds(first, count), pl.ds(start, width)],
                    out.at[:, pl.ds(k * width, width)],
                    sems.at[step, k],
                )
            )
    for copy in copies:
        copy.start()
    for copy in copies:
        copy.wait()


def image_kernel(table, slot_grad, grad_low, image_grad):
    slot_total, keys_img, cols = slot_grad.shape
    image_grad[...] = jnp.zeros_like(image_grad)
    for slot in range(slot_total):
        image = table[slot // CAP, slot % CAP]

        @pl.when(image > 0)
        def _():
            image_grad[image - 1] += slot_grad[slot].astype(F32)

    total = image_grad[...].reshape(image_grad.shape[0] * keys_img, cols)
    grad_low[...] = total.T.astype(BF16)


def near_kernel(place, grad_low, features, *rest):
    sources, (grad_again, rows, sems) = rest[:-3], rest[-3:]
    x_at, z_at, core = place[0], place[1], place[2]
    width = rows.shape[3] // SIDE

    def own_copy(half, k):
        if half == 0:
            start = (x_at * SIDE + k) * (2 * width)
        else:
            start = (k * SIDE + z_at) * (2 * width) + width
        return pltpu.make_async_copy(
            features.at[:, pl.ds(pl.multiple_of(start, width), width)],
            rows.at[half, 0, :, pl.ds(k * width, width)],
            sems.at[half, k],
        )

    def far_copy(half, index, source):
        to = rows.at[half, (1, 2, 2, 3)[index]]
        if index in (1, 2):
            count = source.shape[0]
            first = place[3] if index == 1 else 1 - place[3]
            to = to.at[pl.ds(pl.multiple_of(first * count, count), count)]
        return pltpu.make_async_copy(source, to, sems.at[half, SIDE + index])

    far = len(sources) // 2
    for half in range(2):
        for k in range(SIDE):
            own_copy(half, k).start()
        for at, part in ((half, sources[:far]), (1 - half, sources[far:])):

            @pl.when(core == at)
            def _():
                for step in range(far):
                    far_copy(half, step, part[step]).start()

    grad_again[...] = grad_low[...]
    for half in range(2):
        for k in range(SIDE):
            own_copy(half, k).wait()
        for step in range(far):
            far_copy(half, step, sources[step]).wait()


def weight_kernel(place, *refs, half):
    grads, rows, outs = refs[:SIDE], refs[SIDE], refs[SIDE + 1 :]
    width = rows.shape[3] // SIDE
    for step in range(SIDE):
        start = pl.multiple_of(lax.rem(place[1 - half] + step, SIDE) * width, width)
        total = None
        for index in range(SIDE):
            part = jnp.dot(
                grads[index][...],
                rows[half, index, :, pl.ds(start, width)],
                preferred_element_type=F32,
            )
            total = part if index == 0 else total + part
        outs[step][...] = total.astype(outs[step].dtype)


def final_kernel(*refs):
    out = refs[-1]
    width = refs[0].shape[1]
    for half in range(2):
        own, one, two, three = refs[4 * half : 4 * half + 4]
        total = own[...] + one[...].astype(F32) + two[...].astype(F32) + three[...].astype(F32)
        for kind in range(2):
            out[half * width : (half + 1) * width, kind, :] = total[kind * HD : (kind + 1) * HD].T


def shift(values, axis, step):
    pairs = []
    for x in range(SIDE):
        for z in range(SIDE):
            to = ((x + step) % SIDE, z) if axis == "x" else (x, (z + step) % SIDE)
            pairs.append((x * SIDE + z, to[0] * SIDE + to[1]))
    return lax.ppermute(values, "txt", pairs)


def feature_shift(values, step):
    pairs = []
    for img in range(lax.axis_size("img")):
        for x in range(SIDE):
            for z in range(SIDE):
                to = ((x + step) % SIDE, z) if img % 2 == 0 else (x, (z + step) % SIDE)
                side = SIDE * SIDE
                pairs.append((img * side + x * SIDE + z, img * side + to[0] * SIDE + to[1]))
    return lax.ppermute(values, ("img", "txt"), pairs)


def swap_img(values, bit):
    return lax.ppermute(values, "img", [(i, i ^ bit) for i in range(lax.axis_size("img"))])


def shards(features, tile_count, kv_weight, queries, out_grad, image_ids, text_len):
    txt_count = lax.axis_size("txt")
    shard_index = lax.axis_index("txt")
    img_dev, keys_img, feat_width = features.shape
    seq_dev, picks = image_ids.shape
    head_cols = kv_weight.shape[2]
    cols = 2 * head_cols
    request_total = seq_dev * picks
    slot_total = txt_count * CAP
    whole = pl.BlockSpec(memory_space=pltpu.VMEM)
    scalars = pl.BlockSpec(memory_space=pltpu.SMEM)
    in_hbm = pl.BlockSpec(memory_space=pltpu.HBM)

    def params(mib):
        return pltpu.CompilerParams(vmem_limit_bytes=mib * MIB)


    wanted, meta = pl.pallas_call(
        functools.partial(request_kernel, img_dev=img_dev),
        out_shape=[
            jax.ShapeDtypeStruct((txt_count, 128), jnp.int32),
            jax.ShapeDtypeStruct((2 * request_total,), jnp.int32),
        ],
        in_specs=[scalars, scalars],
        out_specs=[whole, scalars],
        scratch_shapes=[pltpu.SMEM((txt_count,), jnp.int32)],
        name="request_table",
    )(image_ids.T, tile_count)
    table = lax.all_to_all(wanted, "txt", 0, 0, tiled=True)
    place = jnp.stack([shard_index // SIDE, shard_index % SIDE, lax.axis_index("img") % 2, lax.axis_index("img") // 2 % 2])

    flat_features = features.reshape(img_dev * keys_img, feat_width)
    own_pairs = jnp.dot(
        flat_features, kv_weight.reshape(feat_width, cols), preferred_element_type=F32
    ).astype(BF16)
    sent_pairs = pl.pallas_call(
        fill_kernel,
        out_shape=jax.ShapeDtypeStruct((slot_total, keys_img, cols), BF16),
        in_specs=[scalars, whole],
        out_specs=whole,
        compiler_params=params(8),
        name="fill_slots",
    )(table, own_pairs.reshape(img_dev, keys_img, cols))
    got_pairs = lax.all_to_all(
        sent_pairs.reshape(txt_count, CAP, keys_img, cols), "txt", 0, 0, tiled=True
    ).reshape(slot_total, keys_img, cols)

    block = feat_width // txt_count
    width = block // 2
    held_rows = img_dev * keys_img
    held_features = pltpu.with_memory_space_constraint(flat_features, pltpu.HBM)
    messages = pl.pallas_call(
        pack_kernel,
        out_shape=[
            jax.ShapeDtypeStruct((count, SIDE * width), BF16)
            for count in (held_rows, held_rows // 2, held_rows)
        ],
        in_specs=[scalars, in_hbm, in_hbm],
        out_specs=[whole] * (SIDE - 1),
        scratch_shapes=[pltpu.SemaphoreType.DMA((SIDE - 1, SIDE))],
        compiler_params=params(4),
        cost_estimate=pl.CostEstimate(
            flops=0, bytes_accessed=2 * flat_features.size, transcendentals=0
        ),
        name="pack_features",
    )(place, sent_pairs, held_features)
    got_features = [feature_shift(part, step + 1) for step, part in enumerate(messages)]
    got_features.insert(2, swap_img(got_features[1], 2))
    swapped_features = [swap_img(part, 1) for part in got_features]
    attended, grad_query, slot_grad = pl.pallas_call(
        functools.partial(attend_kernel, img_dev=img_dev),
        out_shape=[
            jax.ShapeDtypeStruct(queries.shape, BF16),
            jax.ShapeDtypeStruct(queries.shape, BF16),
            jax.ShapeDtypeStruct((slot_total, keys_img, cols), BF16),
        ],
        in_specs=[scalars, scalars, scalars, in_hbm, in_hbm, whole],
        out_specs=[in_hbm, in_hbm, whole],
        scratch_shapes=[pltpu.VMEM(queries.shape, BF16)] * 4
        + [pltpu.SemaphoreType.DMA((4, seq_dev))],
        compiler_params=params(24),
        name="attend",
    )(meta, table, text_len, *[pltpu.with_memory_space_constraint(x, pltpu.HBM) for x in (queries, out_grad)], got_pairs)
    back_grad = lax.all_to_all(
        slot_grad.reshape(txt_count, CAP, keys_img, cols), "txt", 0, 0, tiled=True
    ).reshape(slot_total, keys_img, cols)

    grad_low = pl.pallas_call(
        image_kernel,
        out_shape=jax.ShapeDtypeStruct((cols, img_dev * keys_img), BF16),
        in_specs=[scalars, whole],
        out_specs=whole,
        scratch_shapes=[pltpu.VMEM((img_dev, keys_img, cols), F32)],
        compiler_params=params(8),
        name="image_grads",
    )(table, back_grad)
    grad_again, near = pl.pallas_call(
        near_kernel,
        out_shape=[
            jax.ShapeDtypeStruct(grad_low.shape, BF16),
            jax.ShapeDtypeStruct((2, SIDE, img_dev * keys_img, SIDE * width), BF16),
        ],
        in_specs=[scalars, whole] + [in_hbm] * (2 * SIDE + 1),
        out_specs=[whole] * 2,
        scratch_shapes=[pltpu.SemaphoreType.DMA((2, 2 * SIDE))],
        compiler_params=params(4),
        cost_estimate=pl.CostEstimate(
            flops=0, bytes_accessed=2 * flat_features.size, transcendentals=0
        ),
        name="near_features",
    )(place, grad_low, held_features, *got_features, *swapped_features)
    along = {
        (half, step): shift(grad_again if (half, step) == (1, 3) else grad_low, "xz"[half], step)
        for step in (2, 1, 3)
        for half in range(2)
    }
    final = []
    for half in range(2):
        own, *others = pl.pallas_call(
            functools.partial(weight_kernel, half=half),
            out_shape=[
                jax.ShapeDtypeStruct((cols, width), F32 if step == 0 else BF16)
                for step in range(SIDE)
            ],
            in_specs=[scalars] + [whole] * (SIDE + 1),
            out_specs=[whole] * SIDE,
            compiler_params=params(8),
            name="weight_part",
        )(place, grad_low, *[along[half, step] for step in range(1, SIDE)], near)
        sent = {step: shift(others[step - 1], "zx"[half], step) for step in (2, 1, 3)}
        final += [own] + [sent[step] for step in range(1, SIDE)]
    weight_grad = pl.pallas_call(
        final_kernel,
        out_shape=jax.ShapeDtypeStruct((block, 2, head_cols), F32),
        in_specs=[whole] * 8,
        out_specs=whole,
        compiler_params=params(8),
        name="weight_total",
    )(*final)
    return attended, grad_query, weight_grad


def solution(mesh):
    in_specs = (
        P("txt", None, None),
        P("txt"),
        P(None, None, "img"),
        P("txt", "img"),
        P("txt", "img"),
        P("txt", None),
        P("txt"),
    )
    out_specs = (P("txt", "img"), P("txt", "img"), P("txt", None, "img"))
    return jax.shard_map(shards, mesh=mesh, in_specs=in_specs, out_specs=out_specs, check_vma=False)
```
